32 devices in a mesh: gx: 8 (over z, y), gy: 4 (over x, core).
Axes of the slice: x: 2, y: 2, z: 4, core: 2. Of those that a mesh axis runs over, the one named last changes fastest.
Arguments:
- members_state: float32 [3, 64, 64, 512], P(None, None, 'gx', 'gy'), may hold values from -6 to 6
- depth_level: int32 [64, 512], P('gx', 'gy'), may hold values from 1 to 8
- land_mask: int32 [64, 512], P('gx', 'gy'), may hold values 0 or 1
- obs_cells: int32 [8, 4, 256], P('gx', 'gy'), may hold values from 0 to 1023
- obs_values: float32 [8, 4, 256], P('gx', 'gy'), may hold values from -6 to 6
- obs_error: float32 [8, 4, 256], P('gx', 'gy'), may hold values from 2 to 8
Outputs:
- analysis: float32 [3, 64, 64, 512], P(None, None, 'gx', 'gy')
The draws below stay inside these ranges and needn't reach their ends.
Inputs may be any that keep to these rules, and one draw needn't show every extreme that they name: Each value of obs_cells is the row-major index of a cell within the 8 x 128 block held by the device at the same position along gx and gy.
All inputs are finite; a program needn't handle non-finite values. No bound on the sum of `land_mask` on one device may be relied on, other than what follows from the above.
Results may differ from the reference program's by a relative error of at most 0.00005.
Values sent between devices are 32-bit elements; how exact they have to be, the bound alone decides.
A program may use at most 64 MiB of HBM per device.

```python
import math
import jax
import jax.numpy as jnp
from jax import lax

MEMBERS = 64
CX = 8
CY = 128
OBS = 256
NX = 64
NY = 512
N_GX = 8
N_GY = 4


def plant(drawn, stream_key, smallest, high):
    extent = drawn.shape
    index_at = [jax.random.randint(jax.random.fold_in(stream_key, axis), (), 0, extent[axis]) for axis in range(len(extent))]
    drawn = drawn.at[tuple(index_at)].set(smallest)
    longest = extent.index(max(extent))
    index_at[longest] = (index_at[longest] + 1) % extent[longest]
    return drawn.at[tuple(index_at)].set(high)


def steps_of(own_key, shape, shards, smallest, largest):
    factor_of, own = 1.0, jax.random.fold_in(own_key, 6)
    for axis_at, blocks in shards:
        steps = jnp.exp(jax.random.uniform(jax.random.fold_in(own, axis_at), (blocks,), jnp.float32, smallest / len(shards), largest / len(shards)))
        factor_of = factor_of * jnp.repeat(steps, shape[axis_at] // blocks).reshape([-1 if axis == axis_at else 1 for axis in range(len(shape))])
    return factor_of


def noise(own_key, shape, spread, limit, pieces=(), held_as=jnp.bfloat16):
    result = spread * jax.random.normal(own_key, shape, jnp.float32)
    if pieces:
        result = result * steps_of(own_key, shape, pieces, -0.22, 0.18)
    return jnp.clip(result, -limit, limit).astype(held_as)


def setup_inputs(seed: int = 0) -> dict:
    streams_of = jax.random.split(jax.random.key(seed), 7)
    members_state = noise(streams_of[0], (3, MEMBERS, NX, NY), 1.0, 6.0, ((2, 8), (3, 4)), jnp.float32)
    depth_level = plant(jax.random.randint(streams_of[1], (NX, NY), 1, 9), jax.random.fold_in(streams_of[1], 1), 1, 8).astype(jnp.int32)
    land_mask = plant((jax.random.randint(streams_of[2], (NX, NY), 0, 8) < 7).astype(jnp.int32), jax.random.fold_in(streams_of[2], 1), 0, 1)
    obs_cells = plant(jax.random.randint(streams_of[3], (N_GX, N_GY, OBS), 0, CX * CY), jax.random.fold_in(streams_of[3], 1), 0, (CX * CY) - 1).astype(jnp.int32)
    obs_values = noise(streams_of[4], (N_GX, N_GY, OBS), 1.0, 6.0, ((0, 8), (1, 4)), jnp.float32)
    obs_error = jnp.clip(jnp.exp(math.log(8.0) - 1.3862944 * jax.random.uniform(streams_of[5], (N_GX, N_GY, OBS), jnp.float32) ** steps_of(streams_of[5], (N_GX, N_GY, OBS), ((0, 8), (1, 4)), -0.2, 0.2)), 2.0, 8.0)
    return dict(members_state=members_state, depth_level=depth_level, land_mask=land_mask, obs_cells=obs_cells, obs_values=obs_values, obs_error=obs_error)


def height_tendency(padded, geo):
    h = padded[0]
    u = padded[1]
    v = padded[2]
    depth = geo[0]
    mask = geo[1][1:-1, 1:-1]
    east = depth * u
    north = depth * v

    def along_x(a):
        return (a[:, 2:, 1:-1] - a[:, :-2, 1:-1]) * 0.5

    def along_y(a):
        return (a[:, 1:-1, 2:] - a[:, 1:-1, :-2]) * 0.5

    def laplace(a):
        return a[:, 2:, 1:-1] + a[:, :-2, 1:-1] + a[:, 1:-1, 2:] + a[:, 1:-1, :-2] - 4.0 * a[:, 1:-1, 1:-1]

    def inner(a):
        return a[:, 1:-1, 1:-1]
    dh = -along_x(east) - along_y(north) + 0.05 * laplace(h)
    du = -along_x(h) + 0.2 * inner(v) + 0.05 * laplace(u)
    dv = -along_y(h) - 0.2 * inner(u) + 0.05 * laplace(v)
    return jnp.stack([dh, du, dv]) * mask

def tri_solve(lower, rhs, flipped):
    return lax.linalg.triangular_solve(lower, rhs, left_side=True, lower=True, transpose_a=flipped)

def reference(members_state, depth_level, land_mask, obs_cells, obs_values, obs_error):
    maskf = land_mask.astype(jnp.float32)
    geo = jnp.stack([0.25 * depth_level.astype(jnp.float32) * maskf, maskf])
    geo_pad = jnp.pad(geo, ((0, 0), (1, 1), (1, 1)))

    def map_through_observer(x):
        return height_tendency(jnp.pad(x, ((0, 0), (0, 0), (1, 1), (1, 1))), geo_pad)
    first_offset = members_state * maskf
    s1 = first_offset + 0.3 * map_through_observer(first_offset)
    variance_estimate2 = 0.75 * first_offset + 0.25 * (s1 + 0.3 * map_through_observer(s1))
    prior_model_vector = 1.0 / 3.0 * first_offset + 2.0 / 3.0 * (variance_estimate2 + 0.3 * map_through_observer(variance_estimate2))
    sample_average = lax.optimization_barrier(jnp.mean(prior_model_vector, axis=1, keepdims=True))
    sample_deviations = prior_model_vector - sample_average
    sample_number = prior_model_vector.shape[1]
    block_x = jnp.arange(N_GX, dtype=jnp.int32)[:, None, None] * CX
    block_y = jnp.arange(N_GY, dtype=jnp.int32)[None, :, None] * CY
    horizontal_sum_across = (block_x + obs_cells // CY).reshape(-1)
    vertical_sum_across = (block_y + obs_cells % CY).reshape(-1)
    measured_data = prior_model_vector[0][:, horizontal_sum_across, vertical_sum_across]
    obs_mean = lax.optimization_barrier(jnp.mean(measured_data, axis=0, keepdims=True))
    error = obs_error.reshape(-1)
    scaled = (measured_data - obs_mean) / (error * jnp.sqrt(jnp.float32(sample_number - 1)))
    innovation = (obs_values.reshape(-1) - obs_mean[0]) / error
    gram = jnp.dot(scaled, scaled.T, precision=lax.Precision.HIGHEST)
    projection = jnp.dot(scaled, innovation, precision=lax.Precision.HIGHEST)
    eye = jnp.eye(sample_number, dtype=jnp.float32)
    lower = jnp.linalg.cholesky(eye + gram)
    half = tri_solve(lower, projection[:, None], False)
    weights = tri_solve(lower, half, True)[:, 0]
    inverse = tri_solve(lower, eye, False)
    transform = weights[:, None] / jnp.sqrt(jnp.float32(sample_number - 1)) + inverse.T
    mixed = jnp.einsum('km,fkxy->fmxy', transform, sample_deviations, precision=lax.Precision.HIGHEST)
    return sample_average + mixed
```

```python
import functools
import math

import jax
import jax.numpy as jnp
from jax import lax
from jax.experimental import pallas as pl
from jax.experimental.pallas import tpu as pltpu
from jax.sharding import PartitionSpec as P

W = 3
CHUNK = 16
F32 = jnp.float32
HIGH = lax.Precision.HIGHEST
NT = (((1,), (1,)), ((), ()))


def lanes(shape):
    return lax.broadcasted_iota(jnp.int32, shape, 1)


def roll(a, by):
    by = by % a.shape[-1]
    return a if by == 0 else pltpu.roll(a, by, a.ndim - 1)


def pack(rows):
    out = jnp.zeros_like(rows[0])
    slot = lanes(out.shape) // 8
    for x, row in enumerate(rows):
        out = jnp.where(slot == x, roll(row, 8 * x + 4), out)
    return out


def west(c, strip, x):
    return jnp.where(lanes(c.shape) == 0, roll(strip, -(8 * x + 3)), roll(c, 1))


def east(c, strip, x):
    last = c.shape[1] - 1
    return jnp.where(lanes(c.shape) == last, roll(strip, last - (8 * x + 4)), roll(c, -1))


def tendency(c, up, dn, lf, rt, h_up, h_dn, h_lf, h_rt, mask):
    def lap(f):
        return up[f] + dn[f] + lf[f] + rt[f] - 4.0 * c[f]

    dh = -0.5 * (h_dn * dn[1] - h_up * up[1]) - 0.5 * (h_rt * rt[2] - h_lf * lf[2]) + 0.05 * lap(0)
    du = -0.5 * (dn[0] - up[0]) + 0.2 * c[2] + 0.05 * lap(1)
    dv = -0.5 * (rt[0] - lf[0]) - 0.2 * c[1] + 0.05 * lap(2)
    return dh * mask, du * mask, dv * mask


def forecast_kernel(
    ngx, ngy, state, depth, land, cells, values, error,
    anom_out, mean_out, red_out,
    y, z1, z2, geo, hl, hr, k, lk, rk, gk, glk, grk, sgeo, part, pred, got, gxbuf,
    row_s, row_r, col_s, col_r, grow_s, grow_r, gcol_s, gcol_r, ps, pr, xs, xr,
):
    members = state.shape[1] // depth.shape[0]
    cx = depth.shape[0]
    cy = depth.shape[1]
    ext = cx + 2 * W
    nc = members // CHUNK
    gx = lax.axis_index("gx")
    gy = lax.axis_index("gy")
    steps = ngx.bit_length() - 1

    def dev(a, b):
        return (a, b)

    bar = pltpu.get_barrier_semaphore()
    count = 0
    for target in (
        [dev(lax.rem(gx + 1, ngx), gy), dev(lax.rem(gx + ngx - 1, ngx), gy)]
        + [dev(gx, lax.rem(gy + d, ngy)) for d in range(1, ngy)]
        + [dev(gx + (1 << s) * (1 - 2 * (lax.rem(gx // (1 << s), 2))), gy) for s in range(steps)]
    ):
        pl.semaphore_signal(bar, inc=1, device_id=target, device_id_type=pl.DeviceIdType.MESH)
        count += 1

    maskf = land[...].astype(F32)
    heights = 0.25 * depth[...].astype(F32) * maskf
    for x in range(cx):
        geo[x + W, 0] = jnp.broadcast_to(heights[x : x + 1], (8, cy))
        geo[x + W, 1] = jnp.broadcast_to(maskf[x : x + 1], (8, cy))
    for c in range(nc):
        for f in range(3):
            for x in range(cx):
                y[c, x + W, f] = (
                    state[f, pl.ds(c * CHUNK * cx + x, CHUNK, stride=cx), :] * maskf[x : x + 1]
                )

    @pl.when(gx == 0)
    def _():
        y[:, 0:W] = jnp.zeros((nc, W, 3, CHUNK, cy), F32)
        geo[0:W] = jnp.zeros((W, 2, 8, cy), F32)

    @pl.when(gx == ngx - 1)
    def _():
        y[:, cx + W :] = jnp.zeros((nc, W, 3, CHUNK, cy), F32)
        geo[cx + W :] = jnp.zeros((W, 2, 8, cy), F32)

    @pl.when(gy == 0)
    def _():
        lk[...] = jnp.zeros(lk.shape, F32)
        glk[...] = jnp.zeros(glk.shape, F32)

    @pl.when(gy == ngy - 1)
    def _():
        rk[...] = jnp.zeros(rk.shape, F32)
        grk[...] = jnp.zeros(grk.shape, F32)

    pl.semaphore_wait(bar, count)

    def copy(src, dst, s, r, target):
        return pltpu.make_async_remote_copy(
            src_ref=src, dst_ref=dst, send_sem=s, recv_sem=r,
            device_id=target, device_id_type=pl.DeviceIdType.MESH,
        )

    below = dev(lax.rem(gx + 1, ngx), gy)
    above = dev(lax.rem(gx + ngx - 1, ngx), gy)
    right = dev(gx, lax.rem(gy + 1, ngy))
    left = dev(gx, lax.rem(gy + ngy - 1, ngy))
    has_up, has_dn = gx > 0, gx < ngx - 1
    has_lf, has_rt = gy > 0, gy < ngy - 1

    def rows_of(ref, s, r):
        return (
            copy(ref.at[pl.ds(cx, W)], ref.at[pl.ds(0, W)], s.at[0], r.at[0], below),
            copy(ref.at[pl.ds(W, W)], ref.at[pl.ds(cx + W, W)], s.at[1], r.at[1], above),
        )

    def cols_of(src, to_left, to_right, s, r):
        return (
            copy(src, to_left, s.at[0], r.at[0], right),
            copy(src, to_right, s.at[1], r.at[1], left),
        )

    def start(pair, first, second):
        pl.when(first)(lambda: pair[0].start())
        pl.when(second)(lambda: pair[1].start())

    def sent(pair, first, second):
        pl.when(first)(lambda: pair[0].wait_send())
        pl.when(second)(lambda: pair[1].wait_send())

    def received(pair, first, second):
        pl.when(second)(lambda: pair[0].wait_recv())
        pl.when(first)(lambda: pair[1].wait_recv())

    geo_rows = rows_of(geo, grow_s, grow_r)
    geo_cols = cols_of(gk, glk, grk, gcol_s, gcol_r)
    member_rows = [rows_of(y.at[c], row_s.at[c], row_r.at[c]) for c in range(nc)]
    member_cols = [cols_of(k.at[c], lk.at[c], rk.at[c], col_s.at[c], col_r.at[c]) for c in range(nc)]
    start(geo_rows, has_dn, has_up)
    for c in range(nc):
        start(member_rows[c], has_dn, has_up)

    root = math.sqrt(members - 1)
    err = error[...]
    cell = cells[...]
    obs = cell.shape[1]
    weight = 1.0 / (err * err * root)
    row_at = cell // cy
    col_at = cell - row_at * cy
    sub = lax.broadcasted_iota(jnp.int32, (cx, obs), 0)
    here = sub == row_at
    by_row = jnp.concatenate(
        [jnp.where(here, weight, 0.0), jnp.where(here, weight * values[...], 0.0)], axis=0
    )
    hot = (lax.broadcasted_iota(jnp.int32, (cy, obs), 0) == col_at).astype(F32)
    sums = lax.dot_general(by_row, hot, NT, precision=HIGH, preferred_element_type=F32)
    s_cell, v_cell = sums[:cx], sums[cx:]

    received(geo_rows, has_dn, has_up)
    for f in range(2):
        gk[f] = pack([geo[x, f] for x in range(ext)])
    start(geo_cols, has_rt, has_lf)

    def strips(c):
        received(member_rows[c], has_dn, has_up)
        for f in range(3):
            k[c, f] = pack([y[c, x, f] for x in range(ext)])
        start(member_cols[c], has_rt, has_lf)

    def sections(c):
        received(member_cols[c], has_rt, has_lf)
        first = lanes((CHUNK, cy)) % 8 < 4
        sl0 = [jnp.where(first, lk[c, f], k[c, f]) for f in range(3)]
        sr0 = [jnp.where(first, k[c, f], rk[c, f]) for f in range(3)]

        def strip_section(s, side):
            return tendency(
                s, [roll(a, 8) for a in s], [roll(a, -8) for a in s],
                [roll(a, 1) for a in s], [roll(a, -1) for a in s],
                sgeo[side, 0, 0:1], sgeo[side, 1, 0:1], sgeo[side, 2, 0:1], sgeo[side, 3, 0:1],
                sgeo[side, 4, 0:1],
            )

        def advance(s, side):
            d = strip_section(s, side)
            one = [s[f] + 0.3 * d[f] for f in range(3)]
            d = strip_section(one, side)
            two = [0.75 * s[f] + 0.25 * (one[f] + 0.3 * d[f]) for f in range(3)]
            return one, two

        sl1, sl2 = advance(sl0, 0)
        sr1, sr2 = advance(sr0, 1)

        def row_section(read, sl, sr, x):
            cc, up, dn = read(x), read(x - 1), read(x + 1)
            lf = [west(cc[f], sl[f], x) for f in range(3)]
            rt = [east(cc[f], sr[f], x) for f in range(3)]
            d = tendency(
                cc, up, dn, lf, rt, geo[x - 1, 0, 0:1], geo[x + 1, 0, 0:1],
                hl[x, 0:1], hr[x, 0:1], geo[x, 1, 0:1],
            )
            return cc, d

        for x in range(1, ext - 1):
            cc, d = row_section(lambda i: [y[c, i, f] for f in range(3)], sl0, sr0, x)
            for f in range(3):
                z1[x, f] = cc[f] + 0.3 * d[f]
        for x in range(2, ext - 2):
            cc, d = row_section(lambda i: [z1[i, f] for f in range(3)], sl1, sr1, x)
            for f in range(3):
                z2[x, f] = 0.75 * y[c, x, f] + 0.25 * (cc[f] + 0.3 * d[f])
        for x in range(3, ext - 3):
            cc, d = row_section(lambda i: [z2[i, f] for f in range(3)], sl2, sr2, x)
            for f in range(3):
                anom_out[f, x - W, c * CHUNK : (c + 1) * CHUNK] = (1.0 / 3.0) * y[c, x, f] + (
                    2.0 / 3.0
                ) * (cc[f] + 0.3 * d[f])

    strips(0)
    received(geo_cols, has_rt, has_lf)
    first = lanes((8, cy)) % 8 < 4
    gl = [jnp.where(first, glk[f], gk[f]) for f in range(2)]
    gr = [jnp.where(first, gk[f], grk[f]) for f in range(2)]
    for side, g in ((0, gl), (1, gr)):
        sgeo[side, 0] = roll(g[0], 8)
        sgeo[side, 1] = roll(g[0], -8)
        sgeo[side, 2] = roll(g[0], 1)
        sgeo[side, 3] = roll(g[0], -1)
        sgeo[side, 4] = g[1]
    for x in range(ext):
        hl[x] = west(geo[x, 0], gl[0], x)
        hr[x] = east(geo[x, 0], gr[0], x)
    for c in range(nc):
        if c + 1 < nc:
            strips(c + 1)
        sections(c)

    gram = jnp.zeros((members + 8, members), F32)
    for f in range(3):
        for x in range(cx):
            full = anom_out[f, x]
            mean = jnp.sum(full, axis=0, keepdims=True) * (1.0 / members)
            mean_out[f, x : x + 1] = mean
            full = full - mean
            anom_out[f, x] = full
            if f == 0:
                wide = full * (s_cell[x : x + 1] * (1.0 / root))
                proj = jnp.broadcast_to(v_cell[x : x + 1] - s_cell[x : x + 1] * mean, (8, cy))
                lhs = jnp.concatenate([wide, proj], axis=0)
                gram += lax.dot_general(lhs, full, NT, precision=HIGH, preferred_element_type=F32)
    half = members // 2
    part[0:half] = jnp.concatenate([gram[:half], gram[half:members]], axis=1)
    part[half:] = jnp.concatenate([gram[members:], gram[members:]], axis=1)

    across = [
        copy(part, got.at[ngy - d - 1], ps.at[d - 1], pr.at[ngy - d - 1], dev(gx, lax.rem(gy + d, ngy)))
        for d in range(1, ngy)
    ]
    for d in across:
        d.start()
    for d in across:
        d.wait_recv()
    total = jnp.zeros(part.shape, F32)
    for b in range(ngy):
        term = part[...]
        for e in range(1, ngy):
            term = jnp.where(lax.rem(gy + e, ngy) == b, got[e - 1], term)
        total = total + term
    for d in across:
        d.wait_send()
    for s in range(steps):
        pred[s] = total
        partner = gx + (1 << s) * (1 - 2 * lax.rem(gx // (1 << s), 2))
        swap = copy(pred.at[s], gxbuf.at[s], xs.at[s], xr.at[s], dev(partner, gy))
        swap.start()
        swap.wait()
        total = total + gxbuf[s]
    red_out[...] = total

    sent(geo_rows, has_dn, has_up)
    sent(geo_cols, has_rt, has_lf)
    for c in range(nc):
        sent(member_rows[c], has_dn, has_up)
        sent(member_cols[c], has_rt, has_lf)


PIVOTS = 4


def analysis_kernel(anom, mean, red, out):
    members = anom.shape[2]
    cx = anom.shape[1]
    half = members // 2
    wide = 2 * members
    packed = red[0:half]
    gram = jnp.concatenate([packed, roll(packed, members)], axis=0)
    lane = lanes((members, wide))
    row = lax.broadcasted_iota(jnp.int32, (members, wide), 0)
    aug = jnp.where(lane < members, gram, 0.0)
    aug = jnp.where((lane == row) | (lane == row + members), aug + 1.0, aug)
    tiles = [aug[8 * t : 8 * t + 8] for t in range(members // 8)]
    sub = lax.broadcasted_iota(jnp.int32, (8, wide), 0)
    for k0 in range(0, members, PIVOTS):
        t0, o = k0 // 8, k0 % 8
        cols = {
            t: [jnp.broadcast_to(tiles[t][:, k0 + j : k0 + j + 1], (8, wide)) for j in range(PIVOTS)]
            for t in range(t0, len(tiles))
        }
        rows = [tiles[t0][o + i : o + i + 1] for i in range(PIVOTS)]
        piv = [[cols[t0][j][o + i : o + i + 1] for j in range(PIVOTS)] for i in range(PIVOTS)]
        inv = []
        for j in range(PIVOTS):
            inv.append(1.0 / piv[j][j])
            for i in range(j + 1, PIVOTS):
                m = piv[i][j] * inv[j]
                rows[i] = rows[i] - m * rows[j]
                for q in range(j + 1, PIVOTS):
                    piv[i][q] = piv[i][q] - m * piv[j][q]
        for t in range(t0, len(tiles)):
            cur = cols[t]
            new = tiles[t]
            for j in range(PIVOTS):
                m = cur[j] * inv[j]
                if t == t0:
                    m = jnp.where(sub >= o + PIVOTS, m, 0.0)
                new = new - m * rows[j]
                for q in range(j + 1, PIVOTS):
                    cur[q] = cur[q] - m * piv[j][q]
            if t == t0:
                for i in range(PIVOTS):
                    new = jnp.where(sub == o + i, rows[i] * lax.rsqrt(piv[i][i]), new)
            tiles[t] = new
    linv = roll(jnp.concatenate(tiles, axis=0), members)[:, :members]
    proj = red[half : half + 1, :members]
    first = jnp.sum(linv * proj, axis=1, keepdims=True)
    weights = jnp.sum(linv * first, axis=0, keepdims=True)
    mix = linv + weights * (1.0 / math.sqrt(members - 1))
    for f in range(3):
        for x in range(cx):
            res = jnp.dot(mix, anom[f, x], precision=HIGH, preferred_element_type=F32)
            out[f, pl.ds(x, members, stride=cx), :] = res + mean[f, x : x + 1]


def local(ngx, ngy, members_state, depth_level, land_mask, obs_cells, obs_values, obs_error):
    _, members, cx, cy = members_state.shape
    obs = obs_cells.shape[-1]
    ext = cx + 2 * W
    nc = members // CHUNK
    steps = ngx.bit_length() - 1
    rows = members // 2 + 8
    vmem = pl.BlockSpec(memory_space=pltpu.VMEM)
    dma = pltpu.SemaphoreType.DMA
    anom, mean, red = pl.pallas_call(
        functools.partial(forecast_kernel, ngx, ngy),
        out_shape=(
            jax.ShapeDtypeStruct((3, cx, members, cy), F32),
            jax.ShapeDtypeStruct((3, cx, cy), F32),
            jax.ShapeDtypeStruct((rows, cy), F32),
        ),
        in_specs=[vmem] * 6,
        out_specs=(vmem,) * 3,
        scratch_shapes=[
            pltpu.VMEM((nc, ext, 3, CHUNK, cy), F32),
            pltpu.VMEM((ext, 3, CHUNK, cy), F32),
            pltpu.VMEM((ext, 3, CHUNK, cy), F32),
            pltpu.VMEM((ext, 2, 8, cy), F32),
            pltpu.VMEM((ext, 8, cy), F32),
            pltpu.VMEM((ext, 8, cy), F32),
            pltpu.VMEM((nc, 3, CHUNK, cy), F32),
            pltpu.VMEM((nc, 3, CHUNK, cy), F32),
            pltpu.VMEM((nc, 3, CHUNK, cy), F32),
            pltpu.VMEM((2, 8, cy), F32),
            pltpu.VMEM((2, 8, cy), F32),
            pltpu.VMEM((2, 8, cy), F32),
            pltpu.VMEM((2, 5, 8, cy), F32),
            pltpu.VMEM((rows, cy), F32),
            pltpu.VMEM((steps, rows, cy), F32),
            pltpu.VMEM((ngy - 1, rows, cy), F32),
            pltpu.VMEM((steps, rows, cy), F32),
            dma((nc, 2)), dma((nc, 2)), dma((nc, 2)), dma((nc, 2)),
            dma((2,)), dma((2,)), dma((2,)), dma((2,)),
            dma((ngy - 1,)), dma((ngy - 1,)), dma((steps,)), dma((steps,)),
        ],
        compiler_params=pltpu.CompilerParams(
            collective_id=0, has_side_effects=True, vmem_limit_bytes=40 * 2**20
        ),
    )(
        members_state.reshape(3, members * cx, cy), depth_level, land_mask,
        obs_cells.reshape(1, obs), obs_values.reshape(1, obs), obs_error.reshape(1, obs),
    )
    out = pl.pallas_call(
        analysis_kernel,
        out_shape=jax.ShapeDtypeStruct((3, members * cx, cy), F32),
        in_specs=[vmem] * 3,
        out_specs=vmem,
        compiler_params=pltpu.CompilerParams(vmem_limit_bytes=40 * 2**20),
    )(anom, mean, red)
    return out.reshape(members_state.shape)


def solution(mesh):
    placed = (
        P(None, None, "gx", "gy"),
        P("gx", "gy"),
        P("gx", "gy"),
        P("gx", "gy", None),
        P("gx", "gy", None),
        P("gx", "gy", None),
    )
    return jax.shard_map(
        functools.partial(local, mesh.shape["gx"], mesh.shape["gy"]),
        mesh=mesh, in_specs=placed, out_specs=P(None, None, "gx", "gy"), check_vma=False,
    )
```

```python
import functools
import math

import jax
import jax.numpy as jnp
from jax import lax
from jax.experimental import pallas as pl
from jax.experimental.pallas import tpu as pltpu
from jax.sharding import PartitionSpec as P

W = 3
CHUNK = 16
F32 = jnp.float32
HIGH = lax.Precision.HIGHEST
NT = (((1,), (1,)), ((), ()))


def lanes(shape):
    return lax.broadcasted_iota(jnp.int32, shape, 1)


def roll(a, by):
    by = by % a.shape[-1]
    return a if by == 0 else pltpu.roll(a, by, a.ndim - 1)


def pack(rows):
    out = jnp.zeros_like(rows[0])
    slot = lanes(out.shape) // 8
    for x, row in enumerate(rows):
        out = jnp.where(slot == x, roll(row, 8 * x + 4), out)
    return out


def west(c, strip, x):
    return jnp.where(lanes(c.shape) == 0, roll(strip, -(8 * x + 3)), roll(c, 1))


def east(c, strip, x):
    last = c.shape[1] - 1
    return jnp.where(lanes(c.shape) == last, roll(strip, last - (8 * x + 4)), roll(c, -1))


def tendency(c, up, dn, lf, rt, h_up, h_dn, h_lf, h_rt, mask):
    def lap(f):
        return up[f] + dn[f] + lf[f] + rt[f] - 4.0 * c[f]

    dh = -0.5 * (h_dn * dn[1] - h_up * up[1]) - 0.5 * (h_rt * rt[2] - h_lf * lf[2]) + 0.05 * lap(0)
    du = -0.5 * (dn[0] - up[0]) + 0.2 * c[2] + 0.05 * lap(1)
    dv = -0.5 * (rt[0] - lf[0]) - 0.2 * c[1] + 0.05 * lap(2)
    return dh * mask, du * mask, dv * mask


def forecast_kernel(
    ngx, ngy, state_hbm, depth_hbm, land_hbm, cells_hbm, values_hbm, error_hbm,
    anom_out, mean_out, red_out,
    state, depth, land, cells, values, error,
    y, z1, z2, spill, geo, hl, hr, k, lk, rk, gk, glk, grk, sgeo, part, pred, got, gxbuf,
    load, row_s, row_r, col_s, col_r, grow_s, grow_r, gcol_s, gcol_r, ps, pr, xs, xr,
):
    cx, cy = depth.shape
    members = state.shape[1] // cx
    ext = cx + 2 * W
    nc = members // CHUNK
    gx = lax.axis_index("gx")
    gy = lax.axis_index("gy")
    steps = ngx.bit_length() - 1

    loads = [
        pltpu.make_async_copy(src, dst, load.at[n])
        for n, (src, dst) in enumerate((
            (depth_hbm, depth), (land_hbm, land), (state_hbm, state),
            (cells_hbm, cells), (values_hbm, values), (error_hbm, error),
        ))
    ]
    for one in loads:
        one.start()

    partners = [gx + (1 << s) * (1 - 2 * lax.rem(gx // (1 << s), 2)) for s in range(steps)]
    greeted = (
        [(lax.rem(gx + 1, ngx), gy), (lax.rem(gx + ngx - 1, ngx), gy)]
        + [(gx, lax.rem(gy + d, ngy)) for d in range(1, ngy)]
        + [(p, gy) for p in partners]
    )
    bar = pltpu.get_barrier_semaphore()
    for target in greeted:
        pl.semaphore_signal(bar, inc=1, device_id=target, device_id_type=pl.DeviceIdType.MESH)

    @pl.when(gx == 0)
    def _():
        spill[:, 0] = jnp.zeros((3, W, members, cy), F32)
        geo[0:W] = jnp.zeros((W, 2, 8, cy), F32)

    @pl.when(gx == ngx - 1)
    def _():
        spill[:, 1] = jnp.zeros((3, W, members, cy), F32)
        geo[cx + W :] = jnp.zeros((W, 2, 8, cy), F32)

    @pl.when(gy == 0)
    def _():
        lk[...] = jnp.zeros(lk.shape, F32)
        glk[...] = jnp.zeros(glk.shape, F32)

    @pl.when(gy == ngy - 1)
    def _():
        rk[...] = jnp.zeros(rk.shape, F32)
        grk[...] = jnp.zeros(grk.shape, F32)

    loads[0].wait()
    loads[1].wait()
    maskf = land[...].astype(F32)
    heights = 0.25 * depth[...].astype(F32) * maskf
    for x in range(cx):
        geo[x + W, 0] = jnp.broadcast_to(heights[x : x + 1], (8, cy))
        geo[x + W, 1] = jnp.broadcast_to(maskf[x : x + 1], (8, cy))

    def copy(src, dst, s, r, target):
        return pltpu.make_async_remote_copy(
            src_ref=src, dst_ref=dst, send_sem=s, recv_sem=r,
            device_id=target, device_id_type=pl.DeviceIdType.MESH,
        )

    below = (lax.rem(gx + 1, ngx), gy)
    above = (lax.rem(gx + ngx - 1, ngx), gy)
    right = (gx, lax.rem(gy + 1, ngy))
    left = (gx, lax.rem(gy + ngy - 1, ngy))
    has_up, has_dn = gx > 0, gx < ngx - 1
    has_lf, has_rt = gy > 0, gy < ngy - 1

    def start(pair, first, second):
        pl.when(first)(lambda: pair[0].start())
        pl.when(second)(lambda: pair[1].start())

    def sent(pair, first, second):
        pl.when(first)(lambda: pair[0].wait_send())
        pl.when(second)(lambda: pair[1].wait_send())

    def received(pair, first, second):
        pl.when(second)(lambda: pair[0].wait_recv())
        pl.when(first)(lambda: pair[1].wait_recv())

    geo_rows = (
        copy(geo.at[pl.ds(cx, W)], geo.at[pl.ds(0, W)], grow_s.at[0], grow_r.at[0], below),
        copy(geo.at[pl.ds(W, W)], geo.at[pl.ds(cx + W, W)], grow_s.at[1], grow_r.at[1], above),
    )
    geo_cols = (
        copy(gk, glk, gcol_s.at[0], gcol_r.at[0], right),
        copy(gk, grk, gcol_s.at[1], gcol_r.at[1], left),
    )
    cols = [
        (
            copy(k.at[c, 1], lk.at[c], col_s.at[c, 0], col_r.at[c, 0], right),
            copy(k.at[c, 0], rk.at[c], col_s.at[c, 1], col_r.at[c, 1], left),
        )
        for c in range(nc)
    ]
    rows = [
        (
            copy(y.at[f, pl.ds(cx + W, W)], spill.at[f, 0], row_s.at[f, 0], row_r.at[f, 0], below),
            copy(y.at[f, pl.ds(0, W)], spill.at[f, 1], row_s.at[f, 1], row_r.at[f, 1], above),
        )
        for f in range(3)
    ]
    pl.semaphore_wait(bar, len(greeted))
    start(geo_rows, has_dn, has_up)

    for one in loads[3:]:
        one.wait()
    root = math.sqrt(members - 1)
    err = error[...]
    cell = cells[...]
    obs = cell.shape[1]
    weight = 1.0 / (err * err * root)
    row_at = cell // cy
    col_at = cell - row_at * cy
    here = lax.broadcasted_iota(jnp.int32, (cx, obs), 0) == row_at
    by_row = jnp.concatenate(
        [jnp.where(here, weight, 0.0), jnp.where(here, weight * values[...], 0.0)], axis=0
    )
    hot = (lax.broadcasted_iota(jnp.int32, (cy, obs), 0) == col_at).astype(F32)
    sums = lax.dot_general(by_row, hot, NT, precision=HIGH, preferred_element_type=F32)
    s_cell, v_cell = sums[:cx], sums[cx:]

    received(geo_rows, has_dn, has_up)
    for f in range(2):
        gk[f] = pack([geo[x, f] for x in range(ext)])
    start(geo_cols, has_rt, has_lf)

    loads[2].wait()
    for f in range(3):
        for x in range(cx):
            y[f, x + W] = state[f, pl.ds(x, members, stride=cx), :] * maskf[x : x + 1]

    received(geo_cols, has_rt, has_lf)
    small = lanes((8, cy)) % 8
    gl = [jnp.where(small < 4, glk[f], gk[f]) for f in range(2)]
    gr = [jnp.where(small < 4, gk[f], grk[f]) for f in range(2)]
    for side, g in ((0, gl), (1, gr)):
        sgeo[side, 0] = roll(g[0], 8)
        sgeo[side, 1] = roll(g[0], -8)
        sgeo[side, 2] = roll(g[0], 1)
        sgeo[side, 3] = roll(g[0], -1)
        sgeo[side, 4] = jnp.where(small == (0, 7)[side], 0.0, g[1])
    for x in range(ext):
        hl[x] = west(geo[x, 0], gl[0], x)
        hr[x] = east(geo[x, 0], gr[0], x)

    zero = jnp.zeros((CHUNK, cy), F32)

    def sections(c):
        at = pl.ds(c * CHUNK, CHUNK)
        inner = lanes((CHUNK, cy)) % 8
        nothing = [zero] * 3
        packed = [
            pack([zero] * W + [y[f, x, at] for x in range(W, W + cx)] + [zero] * W)
            for f in range(3)
        ]

        def strip_section(s, side):
            return tendency(
                s, [roll(a, 8) for a in s], [roll(a, -8) for a in s],
                [roll(a, 1) for a in s], [roll(a, -1) for a in s],
                sgeo[side, 0, 0:1], sgeo[side, 1, 0:1], sgeo[side, 2, 0:1], sgeo[side, 3, 0:1],
                sgeo[side, 4, 0:1],
            )

        def advance(s, side):
            d = strip_section(s, side)
            one = [s[f] + 0.3 * d[f] for f in range(3)]
            d = strip_section(one, side)
            two = [0.75 * s[f] + 0.25 * (one[f] + 0.3 * d[f]) for f in range(3)]
            d = strip_section(two, side)
            for f in range(3):
                k[c, side, f] = (1.0 / 3.0) * s[f] + (2.0 / 3.0) * (two[f] + 0.3 * d[f])
            return one, two

        sl0 = [jnp.where(inner < 4, 0.0, a) for a in packed]
        sr0 = [jnp.where(inner < 4, a, 0.0) for a in packed]
        sl1, sl2 = advance(sl0, 0)
        sr1, sr2 = advance(sr0, 1)
        start(cols[c], has_rt, has_lf)

        def read0(x):
            return [y[f, x, at] for f in range(3)] if W <= x < W + cx else nothing

        def read1(x):
            return [z1[x, f] for f in range(3)] if W - 1 <= x < W + cx + 1 else nothing

        def read2(x):
            return [z2[x, f] for f in range(3)] if W - 2 <= x < W + cx + 2 else nothing

        def row_section(read, reach, sl, sr, x):
            cc, up, dn = read(x), read(x - 1), read(x + 1)
            lf = rt = nothing
            if W - reach <= x < W + cx + reach:
                lf = [west(cc[f], sl[f], x) for f in range(3)]
                rt = [east(cc[f], sr[f], x) for f in range(3)]
            d = tendency(
                cc, up, dn, lf, rt, geo[max(x - 1, 0), 0, 0:1], geo[min(x + 1, ext - 1), 0, 0:1],
                hl[x, 0:1], hr[x, 0:1], geo[x, 1, 0:1],
            )
            return cc, d

        for x in range(2, ext - 2):
            cc, d = row_section(read0, 0, sl0, sr0, x)
            for f in range(3):
                z1[x, f] = cc[f] + 0.3 * d[f]
        for x in range(1, ext - 1):
            cc, d = row_section(read1, 1, sl1, sr1, x)
            begin = read0(x)
            for f in range(3):
                z2[x, f] = 0.75 * begin[f] + 0.25 * (cc[f] + 0.3 * d[f])
        for x in range(ext):
            cc, d = row_section(read2, 2, sl2, sr2, x)
            begin = read0(x)
            for f in range(3):
                y[f, x, at] = (1.0 / 3.0) * begin[f] + (2.0 / 3.0) * (cc[f] + 0.3 * d[f])

    def merge(c, fields):
        at = pl.ds(c * CHUNK, CHUNK)
        lane = lanes((CHUNK, cy))
        edge = (lane < 4) | (lane >= cy - 4)
        for f in fields:
            both = jnp.where(lane % 8 < 4, rk[c, f], lk[c, f])
            for x in range(ext):
                y[f, x, at] = y[f, x, at] + jnp.where(edge, roll(both, -(8 * x + 4)), 0.0)

    for c in range(nc):
        sections(c)
    for c in range(nc):
        received(cols[c], has_rt, has_lf)
        merge(c, (0,))
    start(rows[0], has_dn, has_up)
    for c in range(nc):
        merge(c, (1, 2))
    start(rows[1], has_dn, has_up)
    start(rows[2], has_dn, has_up)

    def whole(f, x):
        full = y[f, x + W]
        if x < W:
            full = full + spill[f, 0, x]
        if x >= cx - W:
            full = full + spill[f, 1, x - (cx - W)]
        mean = jnp.sum(full, axis=0, keepdims=True) * (1.0 / members)
        mean_out[f, x : x + 1] = mean
        full = full - mean
        anom_out[f, x] = full
        return full, mean

    received(rows[0], has_dn, has_up)
    gram = jnp.zeros((members + 8, members), F32)
    for x in range(cx):
        full, mean = whole(0, x)
        wide = full * (s_cell[x : x + 1] * (1.0 / root))
        proj = jnp.broadcast_to(v_cell[x : x + 1] - s_cell[x : x + 1] * mean, (8, cy))
        lhs = jnp.concatenate([wide, proj], axis=0)
        gram += lax.dot_general(lhs, full, NT, precision=HIGH, preferred_element_type=F32)
    half = members // 2
    part[0:half] = jnp.concatenate([gram[:half], gram[half:members]], axis=1)
    part[half:] = jnp.concatenate([gram[members:], gram[members:]], axis=1)

    across = [
        copy(part, got.at[ngy - d - 1], ps.at[d - 1], pr.at[ngy - d - 1], (gx, lax.rem(gy + d, ngy)))
        for d in range(1, ngy)
    ]
    for d in across:
        d.start()
    for d in across:
        d.wait_recv()
    total = jnp.zeros(part.shape, F32)
    for b in range(ngy):
        term = part[...]
        for e in range(1, ngy):
            term = jnp.where(lax.rem(gy + e, ngy) == b, got[e - 1], term)
        total = total + term
    swaps = []
    for s in range(steps):
        pred[s] = total
        swap = copy(pred.at[s], gxbuf.at[s], xs.at[s], xr.at[s], (partners[s], gy))
        swap.start()
        swap.wait_recv()
        swaps.append(swap)
        total = total + gxbuf[s]
    red_out[...] = mixing(total, members)
    for f in (1, 2):
        received(rows[f], has_dn, has_up)
        for x in range(cx):
            whole(f, x)

    for d in across + swaps:
        d.wait_send()
    sent(geo_rows, has_dn, has_up)
    sent(geo_cols, has_rt, has_lf)
    for c in range(nc):
        sent(cols[c], has_rt, has_lf)
    for f in range(3):
        sent(rows[f], has_dn, has_up)


PIVOTS = 4


def mixing(red, members):
    half = members // 2
    wide = 2 * members
    packed = red[0:half]
    gram = jnp.concatenate([packed, roll(packed, members)], axis=0)
    lane = lanes((members, wide))
    row = lax.broadcasted_iota(jnp.int32, (members, wide), 0)
    aug = jnp.where(lane < members, gram, 0.0)
    aug = jnp.where((lane == row) | (lane == row + members), aug + 1.0, aug)
    tiles = [aug[8 * t : 8 * t + 8] for t in range(members // 8)]
    sub = lax.broadcasted_iota(jnp.int32, (8, wide), 0)
    for k0 in range(0, members, PIVOTS):
        t0, o = k0 // 8, k0 % 8
        cols = {
            t: [jnp.broadcast_to(tiles[t][:, k0 + j : k0 + j + 1], (8, wide)) for j in range(PIVOTS)]
            for t in range(t0, len(tiles))
        }
        rows = [tiles[t0][o + i : o + i + 1] for i in range(PIVOTS)]
        piv = [[cols[t0][j][o + i : o + i + 1] for j in range(PIVOTS)] for i in range(PIVOTS)]
        inv = []
        for j in range(PIVOTS):
            inv.append(1.0 / piv[j][j])
            for i in range(j + 1, PIVOTS):
                m = piv[i][j] * inv[j]
                rows[i] = rows[i] - m * rows[j]
                for q in range(j + 1, PIVOTS):
                    piv[i][q] = piv[i][q] - m * piv[j][q]
        for t in range(t0, len(tiles)):
            cur = cols[t]
            new = tiles[t]
            for j in range(PIVOTS):
                m = cur[j] * inv[j]
                if t == t0:
                    m = jnp.where(sub >= o + PIVOTS, m, 0.0)
                new = new - m * rows[j]
                for q in range(j + 1, PIVOTS):
                    cur[q] = cur[q] - m * piv[j][q]
            if t == t0:
                for i in range(PIVOTS):
                    new = jnp.where(sub == o + i, rows[i] * lax.rsqrt(piv[i][i]), new)
            tiles[t] = new
    linv = roll(jnp.concatenate(tiles, axis=0), members)[:, :members]
    proj = red[half : half + 1, :members]
    first = jnp.sum(linv * proj, axis=1, keepdims=True)
    weights = jnp.sum(linv * first, axis=0, keepdims=True)
    mix = linv + weights * (1.0 / math.sqrt(members - 1))
    return mix


def analysis_kernel(anom, mean, mix, out):
    members = anom.shape[2]
    cx = anom.shape[1]
    for f in range(3):
        for x in range(cx):
            res = jnp.dot(mix[...], anom[f, x], precision=HIGH, preferred_element_type=F32)
            out[f, pl.ds(x, members, stride=cx), :] = res + mean[f, x : x + 1]


def local(ngx, ngy, members_state, depth_level, land_mask, obs_cells, obs_values, obs_error):
    _, members, cx, cy = members_state.shape
    obs = obs_cells.shape[-1]
    ext = cx + 2 * W
    nc = members // CHUNK
    steps = ngx.bit_length() - 1
    rows = members // 2 + 8
    vmem = pl.BlockSpec(memory_space=pltpu.VMEM)
    dma = pltpu.SemaphoreType.DMA
    anom, mean, red = pl.pallas_call(
        functools.partial(forecast_kernel, ngx, ngy),
        out_shape=(
            jax.ShapeDtypeStruct((3, cx, members, cy), F32),
            jax.ShapeDtypeStruct((3, cx, cy), F32),
            jax.ShapeDtypeStruct((members, members), F32),
        ),
        in_specs=[pl.BlockSpec(memory_space=pl.ANY)] * 6,
        out_specs=(vmem,) * 3,
        scratch_shapes=[
            pltpu.VMEM((3, members * cx, cy), F32),
            pltpu.VMEM((cx, cy), jnp.int32),
            pltpu.VMEM((cx, cy), jnp.int32),
            pltpu.VMEM((1, obs), jnp.int32),
            pltpu.VMEM((1, obs), F32),
            pltpu.VMEM((1, obs), F32),
            pltpu.VMEM((3, ext, members, cy), F32),
            pltpu.VMEM((ext, 3, CHUNK, cy), F32),
            pltpu.VMEM((ext, 3, CHUNK, cy), F32),
            pltpu.VMEM((3, 2, W, members, cy), F32),
            pltpu.VMEM((ext, 2, 8, cy), F32),
            pltpu.VMEM((ext, 8, cy), F32),
            pltpu.VMEM((ext, 8, cy), F32),
            pltpu.VMEM((nc, 2, 3, CHUNK, cy), F32),
            pltpu.VMEM((nc, 3, CHUNK, cy), F32),
            pltpu.VMEM((nc, 3, CHUNK, cy), F32),
            pltpu.VMEM((2, 8, cy), F32),
            pltpu.VMEM((2, 8, cy), F32),
            pltpu.VMEM((2, 8, cy), F32),
            pltpu.VMEM((2, 5, 8, cy), F32),
            pltpu.VMEM((rows, cy), F32),
            pltpu.VMEM((steps, rows, cy), F32),
            pltpu.VMEM((ngy - 1, rows, cy), F32),
            pltpu.VMEM((steps, rows, cy), F32),
            dma((6,)), dma((3, 2)), dma((3, 2)), dma((nc, 2)), dma((nc, 2)),
            dma((2,)), dma((2,)), dma((2,)), dma((2,)),
            dma((ngy - 1,)), dma((ngy - 1,)), dma((steps,)), dma((steps,)),
        ],
        compiler_params=pltpu.CompilerParams(
            collective_id=0, has_side_effects=True, vmem_limit_bytes=40 * 2**20
        ),
    )(
        members_state.reshape(3, members * cx, cy), depth_level, land_mask,
        obs_cells.reshape(1, obs), obs_values.reshape(1, obs), obs_error.reshape(1, obs),
    )
    out = pl.pallas_call(
        analysis_kernel,
        out_shape=jax.ShapeDtypeStruct((3, members * cx, cy), F32),
        in_specs=[vmem] * 3,
        out_specs=vmem,
        compiler_params=pltpu.CompilerParams(vmem_limit_bytes=40 * 2**20),
    )(anom, mean, red)
    return out.reshape(members_state.shape)


def solution(mesh):
    placed = (
        P(None, None, "gx", "gy"),
        P("gx", "gy"),
        P("gx", "gy"),
        P("gx", "gy", None),
        P("gx", "gy", None),
        P("gx", "gy", None),
    )
    return jax.shard_map(
        functools.partial(local, mesh.shape["gx"], mesh.shape["gy"]),
        mesh=mesh, in_specs=placed, out_specs=P(None, None, "gx", "gy"), check_vma=False,
    )
```

```python
import functools
import math

import jax
import jax.numpy as jnp
from jax import lax
from jax.experimental import pallas as pl
from jax.experimental.pallas import tpu as pltpu
from jax.sharding import PartitionSpec as P

W = 3
CHUNK = 16
F32 = jnp.float32
HIGH = lax.Precision.HIGHEST
NT = (((1,), (1,)), ((), ()))


def lanes(shape):
    return lax.broadcasted_iota(jnp.int32, shape, 1)


def roll(a, by):
    by = by % a.shape[-1]
    return a if by == 0 else pltpu.roll(a, by, a.ndim - 1)


def pack(rows):
    out = jnp.zeros_like(rows[0])
    slot = lanes(out.shape) // 8
    for x, row in enumerate(rows):
        out = jnp.where(slot == x, roll(row, 8 * x + 4), out)
    return out


def edges(strip, x):
    return roll(strip, -(8 * x + 4))


def west(c, edge):
    if edge is None:
        return jnp.where(lanes(c.shape) == 0, 0.0, roll(c, 1))
    return roll(jnp.where(lanes(c.shape) == c.shape[1] - 1, edge, c), 1)


def east(c, edge):
    if edge is None:
        return jnp.where(lanes(c.shape) == c.shape[1] - 1, 0.0, roll(c, -1))
    return roll(jnp.where(lanes(c.shape) == 0, edge, c), -1)


def tendency(c, up, dn, lf, rt, h_up, h_dn, h_lf, h_rt, mask):
    def lap(f):
        return up[f] + dn[f] + lf[f] + rt[f] - 4.0 * c[f]

    dh = -0.5 * (h_dn * dn[1] - h_up * up[1]) - 0.5 * (h_rt * rt[2] - h_lf * lf[2]) + 0.05 * lap(0)
    du = -0.5 * (dn[0] - up[0]) + 0.2 * c[2] + 0.05 * lap(1)
    dv = -0.5 * (rt[0] - lf[0]) - 0.2 * c[1] + 0.05 * lap(2)
    return dh * mask, du * mask, dv * mask


def forecast_kernel(
    ngx, ngy, state_hbm, depth_hbm, land_hbm, cells_hbm, values_hbm, error_hbm,
    anom_out, mean_out, red_out,
    state, depth, land, cells, values, error,
    y, z1, z2, spill, geo, hl, hr, k, lk, rk, gk, glk, grk, sgeo, part, pred, got, gxbuf,
    load, row_s, row_r, col_s, col_r, grow_s, grow_r, gcol_s, gcol_r, ps, pr, xs, xr,
):
    cx, cy = depth.shape
    members = state.shape[1] // cx
    ext = cx + 2 * W
    nc = members // CHUNK
    gx = lax.axis_index("gx")
    gy = lax.axis_index("gy")
    steps = ngx.bit_length() - 1

    loads = [
        pltpu.make_async_copy(src, dst, load.at[n])
        for n, (src, dst) in enumerate((
            (depth_hbm, depth), (land_hbm, land), (state_hbm, state),
            (cells_hbm, cells), (values_hbm, values), (error_hbm, error),
        ))
    ]
    for one in loads:
        one.start()

    partners = [gx + (1 << s) * (1 - 2 * lax.rem(gx // (1 << s), 2)) for s in range(steps)]
    greeted = (
        [(lax.rem(gx + 1, ngx), gy), (lax.rem(gx + ngx - 1, ngx), gy)]
        + [(gx, lax.rem(gy + d, ngy)) for d in range(1, ngy)]
        + [(p, gy) for p in partners]
    )
    bar = pltpu.get_barrier_semaphore()
    for target in greeted:
        pl.semaphore_signal(bar, inc=1, device_id=target, device_id_type=pl.DeviceIdType.MESH)

    @pl.when(gx == 0)
    def _():
        spill[:, 0] = jnp.zeros((3, W, members, cy), F32)
        geo[0:W] = jnp.zeros((W, 2, 8, cy), F32)

    @pl.when(gx == ngx - 1)
    def _():
        spill[:, 1] = jnp.zeros((3, W, members, cy), F32)
        geo[cx + W :] = jnp.zeros((W, 2, 8, cy), F32)

    @pl.when(gy == 0)
    def _():
        lk[...] = jnp.zeros(lk.shape, F32)
        glk[...] = jnp.zeros(glk.shape, F32)

    @pl.when(gy == ngy - 1)
    def _():
        rk[...] = jnp.zeros(rk.shape, F32)
        grk[...] = jnp.zeros(grk.shape, F32)

    loads[0].wait()
    loads[1].wait()
    maskf = land[...].astype(F32)
    heights = 0.25 * depth[...].astype(F32) * maskf
    for x in range(cx):
        geo[x + W, 0] = jnp.broadcast_to(heights[x : x + 1], (8, cy))
        geo[x + W, 1] = jnp.broadcast_to(maskf[x : x + 1], (8, cy))

    def copy(src, dst, s, r, target):
        return pltpu.make_async_remote_copy(
            src_ref=src, dst_ref=dst, send_sem=s, recv_sem=r,
            device_id=target, device_id_type=pl.DeviceIdType.MESH,
        )

    below = (lax.rem(gx + 1, ngx), gy)
    above = (lax.rem(gx + ngx - 1, ngx), gy)
    right = (gx, lax.rem(gy + 1, ngy))
    left = (gx, lax.rem(gy + ngy - 1, ngy))
    has_up, has_dn = gx > 0, gx < ngx - 1
    has_lf, has_rt = gy > 0, gy < ngy - 1

    def start(pair, first, second):
        pl.when(first)(lambda: pair[0].start())
        pl.when(second)(lambda: pair[1].start())

    def sent(pair, first, second):
        pl.when(first)(lambda: pair[0].wait_send())
        pl.when(second)(lambda: pair[1].wait_send())

    def received(pair, first, second):
        pl.when(second)(lambda: pair[0].wait_recv())
        pl.when(first)(lambda: pair[1].wait_recv())

    geo_rows = (
        copy(geo.at[pl.ds(cx, W)], geo.at[pl.ds(0, W)], grow_s.at[0], grow_r.at[0], below),
        copy(geo.at[pl.ds(W, W)], geo.at[pl.ds(cx + W, W)], grow_s.at[1], grow_r.at[1], above),
    )
    geo_cols = (
        copy(gk, glk, gcol_s.at[0], gcol_r.at[0], right),
        copy(gk, grk, gcol_s.at[1], gcol_r.at[1], left),
    )
    cols = [
        (
            copy(k.at[c, 1], lk.at[c], col_s.at[c, 0], col_r.at[c, 0], right),
            copy(k.at[c, 0], rk.at[c], col_s.at[c, 1], col_r.at[c, 1], left),
        )
        for c in range(nc)
    ]
    spans = [(0, c * CHUNK, CHUNK) for c in range(nc)] + [(1, 0, members), (2, 0, members)]
    rows = [
        (
            copy(
                y.at[f, pl.ds(cx + W, W), pl.ds(m, many)], spill.at[f, 0, :, pl.ds(m, many)],
                row_s.at[n, 0], row_r.at[n, 0], below,
            ),
            copy(
                y.at[f, pl.ds(0, W), pl.ds(m, many)], spill.at[f, 1, :, pl.ds(m, many)],
                row_s.at[n, 1], row_r.at[n, 1], above,
            ),
        )
        for n, (f, m, many) in enumerate(spans)
    ]
    pl.semaphore_wait(bar, len(greeted))
    start(geo_rows, has_dn, has_up)

    for one in loads[3:]:
        one.wait()
    root = math.sqrt(members - 1)
    err = error[...]
    cell = cells[...]
    obs = cell.shape[1]
    weight = 1.0 / (err * err * root)
    row_at = cell // cy
    col_at = cell - row_at * cy
    here = lax.broadcasted_iota(jnp.int32, (cx, obs), 0) == row_at
    by_row = jnp.concatenate(
        [jnp.where(here, weight, 0.0), jnp.where(here, weight * values[...], 0.0)], axis=0
    )
    hot = (lax.broadcasted_iota(jnp.int32, (cy, obs), 0) == col_at).astype(F32)
    sums = lax.dot_general(by_row, hot, NT, precision=HIGH, preferred_element_type=F32)
    s_cell, v_cell = sums[:cx], sums[cx:]

    received(geo_rows, has_dn, has_up)
    for f in range(2):
        gk[f] = pack([geo[x, f] for x in range(ext)])
    start(geo_cols, has_rt, has_lf)

    loads[2].wait()
    for f in range(3):
        for x in range(cx):
            y[f, x + W] = state[f, pl.ds(x, members, stride=cx), :] * maskf[x : x + 1]

    received(geo_cols, has_rt, has_lf)
    small = lanes((8, cy)) % 8
    gl = [jnp.where(small < 4, glk[f], gk[f]) for f in range(2)]
    gr = [jnp.where(small < 4, gk[f], grk[f]) for f in range(2)]
    for side, g in ((0, gl), (1, gr)):
        sgeo[side, 0] = roll(g[0], 8)
        sgeo[side, 1] = roll(g[0], -8)
        sgeo[side, 2] = roll(g[0], 1)
        sgeo[side, 3] = roll(g[0], -1)
        sgeo[side, 4] = jnp.where(small == (0, 7)[side], 0.0, g[1])
    for x in range(ext):
        edge = edges(jnp.where(small < 4, gl[0], gr[0]), x)
        hl[x] = west(geo[x, 0], edge)
        hr[x] = east(geo[x, 0], edge)

    zero = jnp.zeros((CHUNK, cy), F32)

    def sections(c):
        at = pl.ds(c * CHUNK, CHUNK)
        inner = lanes((CHUNK, cy)) % 8
        nothing = [zero] * 3
        packed = [
            pack([zero] * W + [y[f, x, at] for x in range(W, W + cx)] + [zero] * W)
            for f in range(3)
        ]

        def strip_section(s, side):
            return tendency(
                s, [roll(a, 8) for a in s], [roll(a, -8) for a in s],
                [roll(a, 1) for a in s], [roll(a, -1) for a in s],
                sgeo[side, 0, 0:1], sgeo[side, 1, 0:1], sgeo[side, 2, 0:1], sgeo[side, 3, 0:1],
                sgeo[side, 4, 0:1],
            )

        def advance(s, side):
            d = strip_section(s, side)
            one = [s[f] + 0.3 * d[f] for f in range(3)]
            d = strip_section(one, side)
            two = [0.75 * s[f] + 0.25 * (one[f] + 0.3 * d[f]) for f in range(3)]
            d = strip_section(two, side)
            for f in range(3):
                k[c, side, f] = (1.0 / 3.0) * s[f] + (2.0 / 3.0) * (two[f] + 0.3 * d[f])
            return one, two

        sl0 = [jnp.where(inner < 4, 0.0, a) for a in packed]
        sr0 = [jnp.where(inner < 4, a, 0.0) for a in packed]
        sl1, sl2 = advance(sl0, 0)
        sr1, sr2 = advance(sr0, 1)
        start(cols[c], has_rt, has_lf)
        strip1 = [jnp.where(inner < 4, l, r) for l, r in zip(sl1, sr1)]
        strip2 = [jnp.where(inner < 4, l, r) for l, r in zip(sl2, sr2)]

        def read0(x):
            return [y[f, x, at] for f in range(3)] if W <= x < W + cx else nothing

        def read1(x):
            return [z1[x, f] for f in range(3)] if W - 1 <= x < W + cx + 1 else nothing

        def read2(x):
            return [z2[x, f] for f in range(3)] if W - 2 <= x < W + cx + 2 else nothing

        def row_section(read, reach, strip, x):
            cc, up, dn = read(x), read(x - 1), read(x + 1)
            lf = rt = nothing
            if W - reach <= x < W + cx + reach:
                edge = [edges(a, x) for a in strip] if strip else [None] * 3
                lf = [west(cc[f], edge[f]) for f in range(3)]
                rt = [east(cc[f], edge[f]) for f in range(3)]
            d = tendency(
                cc, up, dn, lf, rt, geo[max(x - 1, 0), 0, 0:1], geo[min(x + 1, ext - 1), 0, 0:1],
                hl[x, 0:1], hr[x, 0:1], geo[x, 1, 0:1],
            )
            return cc, d

        for x in range(2, ext - 2):
            cc, d = row_section(read0, 0, None, x)
            for f in range(3):
                z1[x, f] = cc[f] + 0.3 * d[f]
        for x in range(1, ext - 1):
            cc, d = row_section(read1, 1, strip1, x)
            begin = read0(x)
            for f in range(3):
                z2[x, f] = 0.75 * begin[f] + 0.25 * (cc[f] + 0.3 * d[f])
        received(cols[c], has_rt, has_lf)
        lane = lanes((CHUNK, cy))
        outer = (lane < 4) | (lane >= cy - 4)
        both = [jnp.where(inner < 4, rk[c, f], lk[c, f]) for f in range(3)]
        for x in range(ext):
            cc, d = row_section(read2, 2, strip2, x)
            begin = read0(x)
            for f in range(3):
                own = (1.0 / 3.0) * begin[f] + (2.0 / 3.0) * (cc[f] + 0.3 * d[f])
                y[f, x, at] = own + jnp.where(outer, edges(both[f], x), 0.0)

    for c in range(nc):
        sections(c)
        start(rows[c], has_dn, has_up)
    for n in range(nc, nc + 2):
        start(rows[n], has_dn, has_up)

    def whole(f, x):
        full = y[f, x + W]
        if x < W:
            full = full + spill[f, 0, x]
        if x >= cx - W:
            full = full + spill[f, 1, x - (cx - W)]
        mean = jnp.sum(full, axis=0, keepdims=True) * (1.0 / members)
        mean_out[f, x : x + 1] = mean
        full = full - mean
        anom_out[f, x] = full
        return full, mean

    for n in range(nc):
        received(rows[n], has_dn, has_up)
    gram = jnp.zeros((members + 8, members), F32)
    for x in range(cx):
        full, mean = whole(0, x)
        wide = full * (s_cell[x : x + 1] * (1.0 / root))
        proj = jnp.broadcast_to(v_cell[x : x + 1] - s_cell[x : x + 1] * mean, (8, cy))
        lhs = jnp.concatenate([wide, proj], axis=0)
        gram += lax.dot_general(lhs, full, NT, precision=HIGH, preferred_element_type=F32)
    half = members // 2
    part[0:half] = jnp.concatenate([gram[:half], gram[half:members]], axis=1)
    part[half:] = jnp.concatenate([gram[members:], gram[members:]], axis=1)

    across = [
        copy(part, got.at[ngy - d - 1], ps.at[d - 1], pr.at[ngy - d - 1], (gx, lax.rem(gy + d, ngy)))
        for d in range(1, ngy)
    ]
    for d in across:
        d.start()
    for d in across:
        d.wait_recv()
    total = jnp.zeros(part.shape, F32)
    for b in range(ngy):
        term = part[...]
        for e in range(1, ngy):
            term = jnp.where(lax.rem(gy + e, ngy) == b, got[e - 1], term)
        total = total + term
    swaps = []
    for s in range(steps):
        pred[s] = total
        swap = copy(pred.at[s], gxbuf.at[s], xs.at[s], xr.at[s], (partners[s], gy))
        swap.start()
        swap.wait_recv()
        swaps.append(swap)
        total = total + gxbuf[s]
    red_out[...] = mixing(total, members)
    for f in (1, 2):
        received(rows[nc + f - 1], has_dn, has_up)
        for x in range(cx):
            whole(f, x)

    for d in across + swaps:
        d.wait_send()
    sent(geo_rows, has_dn, has_up)
    sent(geo_cols, has_rt, has_lf)
    for c in range(nc):
        sent(cols[c], has_rt, has_lf)
    for pair in rows:
        sent(pair, has_dn, has_up)


PIVOTS = 4


def mixing(red, members):
    half = members // 2
    wide = 2 * members
    packed = red[0:half]
    gram = jnp.concatenate([packed, roll(packed, members)], axis=0)
    lane = lanes((members, wide))
    row = lax.broadcasted_iota(jnp.int32, (members, wide), 0)
    aug = jnp.where(lane < members, gram, 0.0)
    aug = jnp.where((lane == row) | (lane == row + members), aug + 1.0, aug)
    tiles = [aug[8 * t : 8 * t + 8] for t in range(members // 8)]
    sub = lax.broadcasted_iota(jnp.int32, (8, wide), 0)
    for k0 in range(0, members, PIVOTS):
        t0, o = k0 // 8, k0 % 8
        cols = {
            t: [jnp.broadcast_to(tiles[t][:, k0 + j : k0 + j + 1], (8, wide)) for j in range(PIVOTS)]
            for t in range(t0, len(tiles))
        }
        rows = [tiles[t0][o + i : o + i + 1] for i in range(PIVOTS)]
        piv = [[cols[t0][j][o + i : o + i + 1] for j in range(PIVOTS)] for i in range(PIVOTS)]
        inv = []
        for j in range(PIVOTS):
            inv.append(1.0 / piv[j][j])
            for i in range(j + 1, PIVOTS):
                m = piv[i][j] * inv[j]
                rows[i] = rows[i] - m * rows[j]
                for q in range(j + 1, PIVOTS):
                    piv[i][q] = piv[i][q] - m * piv[j][q]
        for t in range(t0, len(tiles)):
            cur = cols[t]
            new = tiles[t]
            for j in range(PIVOTS):
                m = cur[j] * inv[j]
                if t == t0:
                    m = jnp.where(sub >= o + PIVOTS, m, 0.0)
                new = new - m * rows[j]
                for q in range(j + 1, PIVOTS):
                    cur[q] = cur[q] - m * piv[j][q]
            if t == t0:
                for i in range(PIVOTS):
                    new = jnp.where(sub == o + i, rows[i] * lax.rsqrt(piv[i][i]), new)
            tiles[t] = new
    linv = roll(jnp.concatenate(tiles, axis=0), members)[:, :members]
    proj = red[half : half + 1, :members]
    first = jnp.sum(linv * proj, axis=1, keepdims=True)
    weights = jnp.sum(linv * first, axis=0, keepdims=True)
    mix = linv + weights * (1.0 / math.sqrt(members - 1))
    return mix


def analysis_kernel(anom, mean, mix, out):
    members = anom.shape[2]
    cx = anom.shape[1]
    for f in range(3):
        for x in range(cx):
            res = jnp.dot(mix[...], anom[f, x], precision=HIGH, preferred_element_type=F32)
            out[f, pl.ds(x, members, stride=cx), :] = res + mean[f, x : x + 1]


def local(ngx, ngy, members_state, depth_level, land_mask, obs_cells, obs_values, obs_error):
    _, members, cx, cy = members_state.shape
    obs = obs_cells.shape[-1]
    ext = cx + 2 * W
    nc = members // CHUNK
    steps = ngx.bit_length() - 1
    rows = members // 2 + 8
    vmem = pl.BlockSpec(memory_space=pltpu.VMEM)
    dma = pltpu.SemaphoreType.DMA
    anom, mean, red = pl.pallas_call(
        functools.partial(forecast_kernel, ngx, ngy),
        out_shape=(
            jax.ShapeDtypeStruct((3, cx, members, cy), F32),
            jax.ShapeDtypeStruct((3, cx, cy), F32),
            jax.ShapeDtypeStruct((members, members), F32),
        ),
        in_specs=[pl.BlockSpec(memory_space=pltpu.HBM)] * 6,
        out_specs=(vmem,) * 3,
        scratch_shapes=[
            pltpu.VMEM((3, members * cx, cy), F32),
            pltpu.VMEM((cx, cy), jnp.int32),
            pltpu.VMEM((cx, cy), jnp.int32),
            pltpu.VMEM((1, obs), jnp.int32),
            pltpu.VMEM((1, obs), F32),
            pltpu.VMEM((1, obs), F32),
            pltpu.VMEM((3, ext, members, cy), F32),
            pltpu.VMEM((ext, 3, CHUNK, cy), F32),
            pltpu.VMEM((ext, 3, CHUNK, cy), F32),
            pltpu.VMEM((3, 2, W, members, cy), F32),
            pltpu.VMEM((ext, 2, 8, cy), F32),
            pltpu.VMEM((ext, 8, cy), F32),
            pltpu.VMEM((ext, 8, cy), F32),
            pltpu.VMEM((nc, 2, 3, CHUNK, cy), F32),
            pltpu.VMEM((nc, 3, CHUNK, cy), F32),
            pltpu.VMEM((nc, 3, CHUNK, cy), F32),
            pltpu.VMEM((2, 8, cy), F32),
            pltpu.VMEM((2, 8, cy), F32),
            pltpu.VMEM((2, 8, cy), F32),
            pltpu.VMEM((2, 5, 8, cy), F32),
            pltpu.VMEM((rows, cy), F32),
            pltpu.VMEM((steps, rows, cy), F32),
            pltpu.VMEM((ngy - 1, rows, cy), F32),
            pltpu.VMEM((steps, rows, cy), F32),
            dma((6,)), dma((nc + 2, 2)), dma((nc + 2, 2)), dma((nc, 2)), dma((nc, 2)),
            dma((2,)), dma((2,)), dma((2,)), dma((2,)),
            dma((ngy - 1,)), dma((ngy - 1,)), dma((steps,)), dma((steps,)),
        ],
        compiler_params=pltpu.CompilerParams(
            collective_id=0, has_side_effects=True, vmem_limit_bytes=40 * 2**20
        ),
    )(
        members_state.reshape(3, members * cx, cy), depth_level, land_mask,
        obs_cells.reshape(1, obs), obs_values.reshape(1, obs), obs_error.reshape(1, obs),
    )
    out = pl.pallas_call(
        analysis_kernel,
        out_shape=jax.ShapeDtypeStruct((3, members * cx, cy), F32),
        in_specs=[vmem] * 3,
        out_specs=vmem,
        compiler_params=pltpu.CompilerParams(vmem_limit_bytes=40 * 2**20),
    )(anom, mean, red)
    return out.reshape(members_state.shape)


def solution(mesh):
    placed = (
        P(None, None, "gx", "gy"),
        P("gx", "gy"),
        P("gx", "gy"),
        P("gx", "gy", None),
        P("gx", "gy", None),
        P("gx", "gy", None),
    )
    return jax.shard_map(
        functools.partial(local, mesh.shape["gx"], mesh.shape["gy"]),
        mesh=mesh, in_specs=placed, out_specs=P(None, None, "gx", "gy"), check_vma=False,
    )
```

```python
import functools
import math

import jax
import jax.numpy as jnp
from jax import lax
from jax.experimental import pallas as pl
from jax.experimental.pallas import tpu as pltpu
from jax.sharding import PartitionSpec as P

W = 3
CHUNK = 16
F32 = jnp.float32
HIGH = lax.Precision.HIGHEST
NT = (((1,), (1,)), ((), ()))


def lanes(shape):
    return lax.broadcasted_iota(jnp.int32, shape, 1)


def roll(a, by):
    by = by % a.shape[-1]
    return a if by == 0 else pltpu.roll(a, by, a.ndim - 1)


def pack(rows):
    out = jnp.zeros_like(rows[0])
    slot = lanes(out.shape) // 8
    for x, row in enumerate(rows):
        out = jnp.where(slot == x, roll(row, 8 * x + 4), out)
    return out


def west(c, strip, x):
    return jnp.where(lanes(c.shape) == 0, roll(strip, -(8 * x + 3)), roll(c, 1))


def east(c, strip, x):
    last = c.shape[1] - 1
    return jnp.where(lanes(c.shape) == last, roll(strip, last - (8 * x + 4)), roll(c, -1))


def tendency(c, up, dn, lf, rt, h_up, h_dn, h_lf, h_rt, mask):
    def lap(f):
        return up[f] + dn[f] + lf[f] + rt[f] - 4.0 * c[f]

    dh = -0.5 * (h_dn * dn[1] - h_up * up[1]) - 0.5 * (h_rt * rt[2] - h_lf * lf[2]) + 0.05 * lap(0)
    du = -0.5 * (dn[0] - up[0]) + 0.2 * c[2] + 0.05 * lap(1)
    dv = -0.5 * (rt[0] - lf[0]) - 0.2 * c[1] + 0.05 * lap(2)
    return dh * mask, du * mask, dv * mask


def forecast_kernel(
    ngx, ngy, state, depth, land, cells, values, error,
    anom_out, mean_out, red_out,
    y, z1, z2, geo, hl, hr, k, lk, rk, gk, glk, grk, sgeo, part, pred, got, gxbuf,
    row_s, row_r, col_s, col_r, grow_s, grow_r, gcol_s, gcol_r, ps, pr, xs, xr,
):
    members = state.shape[1] // depth.shape[0]
    cx = depth.shape[0]
    cy = depth.shape[1]
    ext = cx + 2 * W
    nc = members // CHUNK
    gx = lax.axis_index("gx")
    gy = lax.axis_index("gy")
    steps = ngx.bit_length() - 1

    def dev(a, b):
        return (a, b)

    bar = pltpu.get_barrier_semaphore()
    count = 0
    for target in (
        [dev(lax.rem(gx + 1, ngx), gy), dev(lax.rem(gx + ngx - 1, ngx), gy)]
        + [dev(gx, lax.rem(gy + d, ngy)) for d in range(1, ngy)]
        + [dev(gx + (1 << s) * (1 - 2 * (lax.rem(gx // (1 << s), 2))), gy) for s in range(steps)]
    ):
        pl.semaphore_signal(bar, inc=1, device_id=target, device_id_type=pl.DeviceIdType.MESH)
        count += 1

    maskf = land[...].astype(F32)
    heights = 0.25 * depth[...].astype(F32) * maskf
    for x in range(cx):
        geo[x + W, 0] = jnp.broadcast_to(heights[x : x + 1], (8, cy))
        geo[x + W, 1] = jnp.broadcast_to(maskf[x : x + 1], (8, cy))

    @pl.loop(0, nc)
    def _(c):
        for f in range(3):
            for x in range(cx):
                at = pl.ds(c * CHUNK * cx + x, CHUNK, stride=cx)
                y[c, x + W, f] = state[f, at, :] * maskf[x : x + 1]

    @pl.when(gx == 0)
    def _():
        y[:, 0:W] = jnp.zeros((nc, W, 3, CHUNK, cy), F32)
        geo[0:W] = jnp.zeros((W, 2, 8, cy), F32)

    @pl.when(gx == ngx - 1)
    def _():
        y[:, cx + W :] = jnp.zeros((nc, W, 3, CHUNK, cy), F32)
        geo[cx + W :] = jnp.zeros((W, 2, 8, cy), F32)

    @pl.when(gy == 0)
    def _():
        lk[...] = jnp.zeros(lk.shape, F32)
        glk[...] = jnp.zeros(glk.shape, F32)

    @pl.when(gy == ngy - 1)
    def _():
        rk[...] = jnp.zeros(rk.shape, F32)
        grk[...] = jnp.zeros(grk.shape, F32)

    pl.semaphore_wait(bar, count)

    def copy(src, dst, s, r, target):
        return pltpu.make_async_remote_copy(
            src_ref=src, dst_ref=dst, send_sem=s, recv_sem=r,
            device_id=target, device_id_type=pl.DeviceIdType.MESH,
        )

    below = dev(lax.rem(gx + 1, ngx), gy)
    above = dev(lax.rem(gx + ngx - 1, ngx), gy)
    right = dev(gx, lax.rem(gy + 1, ngy))
    left = dev(gx, lax.rem(gy + ngy - 1, ngy))
    has_up, has_dn = gx > 0, gx < ngx - 1
    has_lf, has_rt = gy > 0, gy < ngy - 1

    def rows_of(ref, s, r):
        return (
            copy(ref.at[pl.ds(cx, W)], ref.at[pl.ds(0, W)], s.at[0], r.at[0], below),
            copy(ref.at[pl.ds(W, W)], ref.at[pl.ds(cx + W, W)], s.at[1], r.at[1], above),
        )

    def cols_of(src, to_left, to_right, s, r):
        return (
            copy(src, to_left, s.at[0], r.at[0], right),
            copy(src, to_right, s.at[1], r.at[1], left),
        )

    def start(pair, first, second):
        pl.when(first)(lambda: pair[0].start())
        pl.when(second)(lambda: pair[1].start())

    def sent(pair, first, second):
        pl.when(first)(lambda: pair[0].wait_send())
        pl.when(second)(lambda: pair[1].wait_send())

    def received(pair, first, second):
        pl.when(second)(lambda: pair[0].wait_recv())
        pl.when(first)(lambda: pair[1].wait_recv())

    geo_rows = rows_of(geo, grow_s, grow_r)
    geo_cols = cols_of(gk, glk, grk, gcol_s, gcol_r)

    def member_rows(c):
        return rows_of(y.at[c], row_s.at[c], row_r.at[c])

    def member_cols(c):
        return cols_of(k.at[c], lk.at[c], rk.at[c], col_s.at[c], col_r.at[c])

    start(geo_rows, has_dn, has_up)

    @pl.loop(0, nc)
    def _(c):
        start(member_rows(c), has_dn, has_up)

    root = math.sqrt(members - 1)
    err = error[...]
    cell = cells[...]
    obs = cell.shape[1]
    weight = 1.0 / (err * err * root)
    row_at = cell // cy
    col_at = cell - row_at * cy
    sub = lax.broadcasted_iota(jnp.int32, (cx, obs), 0)
    here = sub == row_at
    by_row = jnp.concatenate(
        [jnp.where(here, weight, 0.0), jnp.where(here, weight * values[...], 0.0)], axis=0
    )
    hot = (lax.broadcasted_iota(jnp.int32, (cy, obs), 0) == col_at).astype(F32)
    sums = lax.dot_general(by_row, hot, NT, precision=HIGH, preferred_element_type=F32)
    s_cell, v_cell = sums[:cx], sums[cx:]

    received(geo_rows, has_dn, has_up)
    for f in range(2):
        gk[f] = pack([geo[x, f] for x in range(ext)])
    start(geo_cols, has_rt, has_lf)

    def strips(c):
        received(member_rows(c), has_dn, has_up)
        for f in range(3):
            k[c, f] = pack([y[c, x, f] for x in range(ext)])
        start(member_cols(c), has_rt, has_lf)

    def sections(c):
        received(member_cols(c), has_rt, has_lf)
        first = lanes((CHUNK, cy)) % 8 < 4
        sl0 = [jnp.where(first, lk[c, f], k[c, f]) for f in range(3)]
        sr0 = [jnp.where(first, k[c, f], rk[c, f]) for f in range(3)]

        def strip_section(s, side):
            return tendency(
                s, [roll(a, 8) for a in s], [roll(a, -8) for a in s],
                [roll(a, 1) for a in s], [roll(a, -1) for a in s],
                sgeo[side, 0, 0:1], sgeo[side, 1, 0:1], sgeo[side, 2, 0:1], sgeo[side, 3, 0:1],
                sgeo[side, 4, 0:1],
            )

        def advance(s, side):
            d = strip_section(s, side)
            one = [s[f] + 0.3 * d[f] for f in range(3)]
            d = strip_section(one, side)
            two = [0.75 * s[f] + 0.25 * (one[f] + 0.3 * d[f]) for f in range(3)]
            return one, two

        sl1, sl2 = advance(sl0, 0)
        sr1, sr2 = advance(sr0, 1)

        def row_section(read, sl, sr, x):
            cc, up, dn = read(x), read(x - 1), read(x + 1)
            lf = [west(cc[f], sl[f], x) for f in range(3)]
            rt = [east(cc[f], sr[f], x) for f in range(3)]
            d = tendency(
                cc, up, dn, lf, rt, geo[x - 1, 0, 0:1], geo[x + 1, 0, 0:1],
                hl[x, 0:1], hr[x, 0:1], geo[x, 1, 0:1],
            )
            return cc, d

        for x in range(1, ext - 1):
            cc, d = row_section(lambda i: [y[c, i, f] for f in range(3)], sl0, sr0, x)
            for f in range(3):
                z1[x, f] = cc[f] + 0.3 * d[f]
        for x in range(2, ext - 2):
            cc, d = row_section(lambda i: [z1[i, f] for f in range(3)], sl1, sr1, x)
            for f in range(3):
                z2[x, f] = 0.75 * y[c, x, f] + 0.25 * (cc[f] + 0.3 * d[f])
        for x in range(3, ext - 3):
            cc, d = row_section(lambda i: [z2[i, f] for f in range(3)], sl2, sr2, x)
            for f in range(3):
                anom_out[f, x - W, pl.ds(pl.multiple_of(c * CHUNK, CHUNK), CHUNK)] = (1.0 / 3.0) * y[c, x, f] + (
                    2.0 / 3.0
                ) * (cc[f] + 0.3 * d[f])

    strips(0)
    received(geo_cols, has_rt, has_lf)
    first = lanes((8, cy)) % 8 < 4
    gl = [jnp.where(first, glk[f], gk[f]) for f in range(2)]
    gr = [jnp.where(first, gk[f], grk[f]) for f in range(2)]
    for side, g in ((0, gl), (1, gr)):
        sgeo[side, 0] = roll(g[0], 8)
        sgeo[side, 1] = roll(g[0], -8)
        sgeo[side, 2] = roll(g[0], 1)
        sgeo[side, 3] = roll(g[0], -1)
        sgeo[side, 4] = g[1]
    for x in range(ext):
        hl[x] = west(geo[x, 0], gl[0], x)
        hr[x] = east(geo[x, 0], gr[0], x)

    @pl.loop(0, nc)
    def _(c):
        pl.when(c + 1 < nc)(lambda: strips(c + 1))
        sections(c)

    gram = jnp.zeros((members + 8, members), F32)
    for f in range(3):
        for x in range(cx):
            full = anom_out[f, x]
            mean = jnp.sum(full, axis=0, keepdims=True) * (1.0 / members)
            mean_out[f, x : x + 1] = mean
            full = full - mean
            anom_out[f, x] = full
            if f == 0:
                wide = full * (s_cell[x : x + 1] * (1.0 / root))
                proj = jnp.broadcast_to(v_cell[x : x + 1] - s_cell[x : x + 1] * mean, (8, cy))
                lhs = jnp.concatenate([wide, proj], axis=0)
                gram += lax.dot_general(lhs, full, NT, precision=HIGH, preferred_element_type=F32)
    half = members // 2
    part[0:half] = jnp.concatenate([gram[:half], gram[half:members]], axis=1)
    part[half:] = jnp.concatenate([gram[members:], gram[members:]], axis=1)

    across = [
        copy(part, got.at[ngy - d - 1], ps.at[d - 1], pr.at[ngy - d - 1], dev(gx, lax.rem(gy + d, ngy)))
        for d in range(1, ngy)
    ]
    for d in across:
        d.start()
    for d in across:
        d.wait_recv()
    total = jnp.zeros(part.shape, F32)
    for b in range(ngy):
        term = part[...]
        for e in range(1, ngy):
            term = jnp.where(lax.rem(gy + e, ngy) == b, got[e - 1], term)
        total = total + term
    for d in across:
        d.wait_send()
    for s in range(steps):
        pred[s] = total
        partner = gx + (1 << s) * (1 - 2 * lax.rem(gx // (1 << s), 2))
        swap = copy(pred.at[s], gxbuf.at[s], xs.at[s], xr.at[s], dev(partner, gy))
        swap.start()
        swap.wait()
        total = total + gxbuf[s]
    red_out[...] = total

    sent(geo_rows, has_dn, has_up)
    sent(geo_cols, has_rt, has_lf)

    @pl.loop(0, nc)
    def _(c):
        sent(member_rows(c), has_dn, has_up)
        sent(member_cols(c), has_rt, has_lf)


PIVOTS = 4


def analysis_kernel(anom, mean, red, out):
    members = anom.shape[2]
    cx = anom.shape[1]
    half = members // 2
    wide = 2 * members
    packed = red[0:half]
    gram = jnp.concatenate([packed, roll(packed, members)], axis=0)
    lane = lanes((members, wide))
    row = lax.broadcasted_iota(jnp.int32, (members, wide), 0)
    aug = jnp.where(lane < members, gram, 0.0)
    aug = jnp.where((lane == row) | (lane == row + members), aug + 1.0, aug)
    tiles = [aug[8 * t : 8 * t + 8] for t in range(members // 8)]
    sub = lax.broadcasted_iota(jnp.int32, (8, wide), 0)
    for k0 in range(0, members, PIVOTS):
        t0, o = k0 // 8, k0 % 8
        cols = {
            t: [jnp.broadcast_to(tiles[t][:, k0 + j : k0 + j + 1], (8, wide)) for j in range(PIVOTS)]
            for t in range(t0, len(tiles))
        }
        rows = [tiles[t0][o + i : o + i + 1] for i in range(PIVOTS)]
        piv = [[cols[t0][j][o + i : o + i + 1] for j in range(PIVOTS)] for i in range(PIVOTS)]
        inv = []
        for j in range(PIVOTS):
            inv.append(1.0 / piv[j][j])
            for i in range(j + 1, PIVOTS):
                m = piv[i][j] * inv[j]
                rows[i] = rows[i] - m * rows[j]
                for q in range(j + 1, PIVOTS):
                    piv[i][q] = piv[i][q] - m * piv[j][q]
        for t in range(t0, len(tiles)):
            cur = cols[t]
            new = tiles[t]
            for j in range(PIVOTS):
                m = cur[j] * inv[j]
                if t == t0:
                    m = jnp.where(sub >= o + PIVOTS, m, 0.0)
                new = new - m * rows[j]
                for q in range(j + 1, PIVOTS):
                    cur[q] = cur[q] - m * piv[j][q]
            if t == t0:
                for i in range(PIVOTS):
                    new = jnp.where(sub == o + i, rows[i] * lax.rsqrt(piv[i][i]), new)
            tiles[t] = new
    linv = roll(jnp.concatenate(tiles, axis=0), members)[:, :members]
    proj = red[half : half + 1, :members]
    first = jnp.sum(linv * proj, axis=1, keepdims=True)
    weights = jnp.sum(linv * first, axis=0, keepdims=True)
    mix = linv + weights * (1.0 / math.sqrt(members - 1))
    for f in range(3):
        for x in range(cx):
            res = jnp.dot(mix, anom[f, x], precision=HIGH, preferred_element_type=F32)
            out[f, pl.ds(x, members, stride=cx), :] = res + mean[f, x : x + 1]


def local(ngx, ngy, members_state, depth_level, land_mask, obs_cells, obs_values, obs_error):
    _, members, cx, cy = members_state.shape
    obs = obs_cells.shape[-1]
    ext = cx + 2 * W
    nc = members // CHUNK
    steps = ngx.bit_length() - 1
    rows = members // 2 + 8
    vmem = pl.BlockSpec(memory_space=pltpu.VMEM)
    dma = pltpu.SemaphoreType.DMA
    anom, mean, red = pl.pallas_call(
        functools.partial(forecast_kernel, ngx, ngy),
        out_shape=(
            jax.ShapeDtypeStruct((3, cx, members, cy), F32),
            jax.ShapeDtypeStruct((3, cx, cy), F32),
            jax.ShapeDtypeStruct((rows, cy), F32),
        ),
        in_specs=[vmem] * 6,
        out_specs=(vmem,) * 3,
        scratch_shapes=[
            pltpu.VMEM((nc, ext, 3, CHUNK, cy), F32),
            pltpu.VMEM((ext, 3, CHUNK, cy), F32),
            pltpu.VMEM((ext, 3, CHUNK, cy), F32),
            pltpu.VMEM((ext, 2, 8, cy), F32),
            pltpu.VMEM((ext, 8, cy), F32),
            pltpu.VMEM((ext, 8, cy), F32),
            pltpu.VMEM((nc, 3, CHUNK, cy), F32),
            pltpu.VMEM((nc, 3, CHUNK, cy), F32),
            pltpu.VMEM((nc, 3, CHUNK, cy), F32),
            pltpu.VMEM((2, 8, cy), F32),
            pltpu.VMEM((2, 8, cy), F32),
            pltpu.VMEM((2, 8, cy), F32),
            pltpu.VMEM((2, 5, 8, cy), F32),
            pltpu.VMEM((rows, cy), F32),
            pltpu.VMEM((steps, rows, cy), F32),
            pltpu.VMEM((ngy - 1, rows, cy), F32),
            pltpu.VMEM((steps, rows, cy), F32),
            dma((nc, 2)), dma((nc, 2)), dma((nc, 2)), dma((nc, 2)),
            dma((2,)), dma((2,)), dma((2,)), dma((2,)),
            dma((ngy - 1,)), dma((ngy - 1,)), dma((steps,)), dma((steps,)),
        ],
        compiler_params=pltpu.CompilerParams(
            collective_id=0, has_side_effects=True, vmem_limit_bytes=40 * 2**20
        ),
    )(
        members_state.reshape(3, members * cx, cy), depth_level, land_mask,
        obs_cells.reshape(1, obs), obs_values.reshape(1, obs), obs_error.reshape(1, obs),
    )
    out = pl.pallas_call(
        analysis_kernel,
        out_shape=jax.ShapeDtypeStruct((3, members * cx, cy), F32),
        in_specs=[vmem] * 3,
        out_specs=vmem,
        compiler_params=pltpu.CompilerParams(vmem_limit_bytes=40 * 2**20),
    )(anom, mean, red)
    return out.reshape(members_state.shape)


def solution(mesh):
    placed = (
        P(None, None, "gx", "gy"),
        P("gx", "gy"),
        P("gx", "gy"),
        P("gx", "gy", None),
        P("gx", "gy", None),
        P("gx", "gy", None),
    )
    return jax.shard_map(
        functools.partial(local, mesh.shape["gx"], mesh.shape["gy"]),
        mesh=mesh, in_specs=placed, out_specs=P(None, None, "gx", "gy"), check_vma=False,
    )
```

```python
import functools
import math

import jax
import jax.numpy as jnp
from jax import lax
from jax.experimental import pallas as pl
from jax.experimental.pallas import tpu as pltpu
from jax.sharding import PartitionSpec as P

W = 3
CHUNK = 32
F32 = jnp.float32
HIGH = lax.Precision.HIGHEST
NT = (((1,), (1,)), ((), ()))


def lanes(shape):
    return lax.broadcasted_iota(jnp.int32, shape, 1)


def roll(a, by):
    by = by % a.shape[-1]
    return a if by == 0 else pltpu.roll(a, by, a.ndim - 1)


def pack(rows):
    out = jnp.zeros_like(rows[0])
    slot = lanes(out.shape) // 8
    for x, row in enumerate(rows):
        out = jnp.where(slot == x, roll(row, 8 * x + 4), out)
    return out


def west(c, strip, x):
    return jnp.where(lanes(c.shape) == 0, roll(strip, -(8 * x + 3)), roll(c, 1))


def east(c, strip, x):
    last = c.shape[1] - 1
    return jnp.where(lanes(c.shape) == last, roll(strip, last - (8 * x + 4)), roll(c, -1))


def tendency(c, up, dn, lf, rt, h_up, h_dn, h_lf, h_rt, mask):
    def lap(f):
        return up[f] + dn[f] + lf[f] + rt[f] - 4.0 * c[f]

    dh = -0.5 * (h_dn * dn[1] - h_up * up[1]) - 0.5 * (h_rt * rt[2] - h_lf * lf[2]) + 0.05 * lap(0)
    du = -0.5 * (dn[0] - up[0]) + 0.2 * c[2] + 0.05 * lap(1)
    dv = -0.5 * (rt[0] - lf[0]) - 0.2 * c[1] + 0.05 * lap(2)
    return dh * mask, du * mask, dv * mask


def forecast_kernel(
    ngx, ngy, state, depth, land, cells, values, error,
    anom_out, mean_out, red_out,
    y, z1, z2, geo, hl, hr, k, lk, rk, gk, glk, grk, sgeo, part, pred, got, gxbuf,
    row_s, row_r, col_s, col_r, grow_s, grow_r, gcol_s, gcol_r, ps, pr, xs, xr,
):
    members = state.shape[1] // depth.shape[0]
    cx = depth.shape[0]
    cy = depth.shape[1]
    ext = cx + 2 * W
    nc = members // CHUNK
    gx = lax.axis_index("gx")
    gy = lax.axis_index("gy")
    steps = ngx.bit_length() - 1

    def dev(a, b):
        return (a, b)

    bar = pltpu.get_barrier_semaphore()
    count = 0
    for target in (
        [dev(lax.rem(gx + 1, ngx), gy), dev(lax.rem(gx + ngx - 1, ngx), gy)]
        + [dev(gx, lax.rem(gy + d, ngy)) for d in range(1, ngy)]
        + [dev(gx + (1 << s) * (1 - 2 * (lax.rem(gx // (1 << s), 2))), gy) for s in range(steps)]
    ):
        pl.semaphore_signal(bar, inc=1, device_id=target, device_id_type=pl.DeviceIdType.MESH)
        count += 1

    maskf = land[...].astype(F32)
    heights = 0.25 * depth[...].astype(F32) * maskf
    for x in range(cx):
        geo[x + W, 0] = jnp.broadcast_to(heights[x : x + 1], (8, cy))
        geo[x + W, 1] = jnp.broadcast_to(maskf[x : x + 1], (8, cy))
    for c in range(nc):
        for f in range(3):
            for x in range(cx):
                y[c, x + W, f] = (
                    state[f, pl.ds(c * CHUNK * cx + x, CHUNK, stride=cx), :] * maskf[x : x + 1]
                )

    @pl.when(gx == 0)
    def _():
        y[:, 0:W] = jnp.zeros((nc, W, 3, CHUNK, cy), F32)
        geo[0:W] = jnp.zeros((W, 2, 8, cy), F32)

    @pl.when(gx == ngx - 1)
    def _():
        y[:, cx + W :] = jnp.zeros((nc, W, 3, CHUNK, cy), F32)
        geo[cx + W :] = jnp.zeros((W, 2, 8, cy), F32)

    @pl.when(gy == 0)
    def _():
        lk[...] = jnp.zeros(lk.shape, F32)
        glk[...] = jnp.zeros(glk.shape, F32)

    @pl.when(gy == ngy - 1)
    def _():
        rk[...] = jnp.zeros(rk.shape, F32)
        grk[...] = jnp.zeros(grk.shape, F32)

    pl.semaphore_wait(bar, count)

    def copy(src, dst, s, r, target):
        return pltpu.make_async_remote_copy(
            src_ref=src, dst_ref=dst, send_sem=s, recv_sem=r,
            device_id=target, device_id_type=pl.DeviceIdType.MESH,
        )

    below = dev(lax.rem(gx + 1, ngx), gy)
    above = dev(lax.rem(gx + ngx - 1, ngx), gy)
    right = dev(gx, lax.rem(gy + 1, ngy))
    left = dev(gx, lax.rem(gy + ngy - 1, ngy))
    has_up, has_dn = gx > 0, gx < ngx - 1
    has_lf, has_rt = gy > 0, gy < ngy - 1

    def rows_of(ref, s, r):
        return (
            copy(ref.at[pl.ds(cx, W)], ref.at[pl.ds(0, W)], s.at[0], r.at[0], below),
            copy(ref.at[pl.ds(W, W)], ref.at[pl.ds(cx + W, W)], s.at[1], r.at[1], above),
        )

    def cols_of(src, to_left, to_right, s, r):
        return (
            copy(src, to_left, s.at[0], r.at[0], right),
            copy(src, to_right, s.at[1], r.at[1], left),
        )

    def start(pair, first, second):
        pl.when(first)(lambda: pair[0].start())
        pl.when(second)(lambda: pair[1].start())

    def sent(pair, first, second):
        pl.when(first)(lambda: pair[0].wait_send())
        pl.when(second)(lambda: pair[1].wait_send())

    def received(pair, first, second):
        pl.when(second)(lambda: pair[0].wait_recv())
        pl.when(first)(lambda: pair[1].wait_recv())

    geo_rows = rows_of(geo, grow_s, grow_r)
    geo_cols = cols_of(gk, glk, grk, gcol_s, gcol_r)
    member_rows = [rows_of(y.at[c], row_s.at[c], row_r.at[c]) for c in range(nc)]
    member_cols = [cols_of(k.at[c], lk.at[c], rk.at[c], col_s.at[c], col_r.at[c]) for c in range(nc)]
    start(geo_rows, has_dn, has_up)
    for c in range(nc):
        start(member_rows[c], has_dn, has_up)

    root = math.sqrt(members - 1)
    err = error[...]
    cell = cells[...]
    obs = cell.shape[1]
    weight = 1.0 / (err * err * root)
    row_at = cell // cy
    col_at = cell - row_at * cy
    sub = lax.broadcasted_iota(jnp.int32, (cx, obs), 0)
    here = sub == row_at
    by_row = jnp.concatenate(
        [jnp.where(here, weight, 0.0), jnp.where(here, weight * values[...], 0.0)], axis=0
    )
    hot = (lax.broadcasted_iota(jnp.int32, (cy, obs), 0) == col_at).astype(F32)
    sums = lax.dot_general(by_row, hot, NT, precision=HIGH, preferred_element_type=F32)
    s_cell, v_cell = sums[:cx], sums[cx:]

    received(geo_rows, has_dn, has_up)
    for f in range(2):
        gk[f] = pack([geo[x, f] for x in range(ext)])
    start(geo_cols, has_rt, has_lf)

    def strips(c):
        received(member_rows[c], has_dn, has_up)
        for f in range(3):
            k[c, f] = pack([y[c, x, f] for x in range(ext)])
        start(member_cols[c], has_rt, has_lf)

    def sections(c):
        received(member_cols[c], has_rt, has_lf)
        first = lanes((CHUNK, cy)) % 8 < 4
        sl0 = [jnp.where(first, lk[c, f], k[c, f]) for f in range(3)]
        sr0 = [jnp.where(first, k[c, f], rk[c, f]) for f in range(3)]

        def strip_section(s, side):
            return tendency(
                s, [roll(a, 8) for a in s], [roll(a, -8) for a in s],
                [roll(a, 1) for a in s], [roll(a, -1) for a in s],
                sgeo[side, 0, 0:1], sgeo[side, 1, 0:1], sgeo[side, 2, 0:1], sgeo[side, 3, 0:1],
                sgeo[side, 4, 0:1],
            )

        def advance(s, side):
            d = strip_section(s, side)
            one = [s[f] + 0.3 * d[f] for f in range(3)]
            d = strip_section(one, side)
            two = [0.75 * s[f] + 0.25 * (one[f] + 0.3 * d[f]) for f in range(3)]
            return one, two

        sl1, sl2 = advance(sl0, 0)
        sr1, sr2 = advance(sr0, 1)

        def row_section(read, sl, sr, x):
            cc, up, dn = read(x), read(x - 1), read(x + 1)
            lf = [west(cc[f], sl[f], x) for f in range(3)]
            rt = [east(cc[f], sr[f], x) for f in range(3)]
            d = tendency(
                cc, up, dn, lf, rt, geo[x - 1, 0, 0:1], geo[x + 1, 0, 0:1],
                hl[x, 0:1], hr[x, 0:1], geo[x, 1, 0:1],
            )
            return cc, d

        for x in range(1, ext - 1):
            cc, d = row_section(lambda i: [y[c, i, f] for f in range(3)], sl0, sr0, x)
            for f in range(3):
                z1[x, f] = cc[f] + 0.3 * d[f]
        for x in range(2, ext - 2):
            cc, d = row_section(lambda i: [z1[i, f] for f in range(3)], sl1, sr1, x)
            for f in range(3):
                z2[x, f] = 0.75 * y[c, x, f] + 0.25 * (cc[f] + 0.3 * d[f])
        for x in range(3, ext - 3):
            cc, d = row_section(lambda i: [z2[i, f] for f in range(3)], sl2, sr2, x)
            for f in range(3):
                anom_out[f, x - W, c * CHUNK : (c + 1) * CHUNK] = (1.0 / 3.0) * y[c, x, f] + (
                    2.0 / 3.0
                ) * (cc[f] + 0.3 * d[f])

    strips(0)
    received(geo_cols, has_rt, has_lf)
    first = lanes((8, cy)) % 8 < 4
    gl = [jnp.where(first, glk[f], gk[f]) for f in range(2)]
    gr = [jnp.where(first, gk[f], grk[f]) for f in range(2)]
    for side, g in ((0, gl), (1, gr)):
        sgeo[side, 0] = roll(g[0], 8)
        sgeo[side, 1] = roll(g[0], -8)
        sgeo[side, 2] = roll(g[0], 1)
        sgeo[side, 3] = roll(g[0], -1)
        sgeo[side, 4] = g[1]
    for x in range(ext):
        hl[x] = west(geo[x, 0], gl[0], x)
        hr[x] = east(geo[x, 0], gr[0], x)
    for c in range(nc):
        if c + 1 < nc:
            strips(c + 1)
        sections(c)

    gram = jnp.zeros((members + 8, members), F32)
    for f in range(3):
        for x in range(cx):
            full = anom_out[f, x]
            mean = jnp.sum(full, axis=0, keepdims=True) * (1.0 / members)
            mean_out[f, x : x + 1] = mean
            full = full - mean
            anom_out[f, x] = full
            if f == 0:
                wide = full * (s_cell[x : x + 1] * (1.0 / root))
                proj = jnp.broadcast_to(v_cell[x : x + 1] - s_cell[x : x + 1] * mean, (8, cy))
                lhs = jnp.concatenate([wide, proj], axis=0)
                gram += lax.dot_general(lhs, full, NT, precision=HIGH, preferred_element_type=F32)
    half = members // 2
    part[0:half] = jnp.concatenate([gram[:half], gram[half:members]], axis=1)
    part[half:] = jnp.concatenate([gram[members:], gram[members:]], axis=1)

    across = [
        copy(part, got.at[ngy - d - 1], ps.at[d - 1], pr.at[ngy - d - 1], dev(gx, lax.rem(gy + d, ngy)))
        for d in range(1, ngy)
    ]
    for d in across:
        d.start()
    for d in across:
        d.wait_recv()
    total = jnp.zeros(part.shape, F32)
    for b in range(ngy):
        term = part[...]
        for e in range(1, ngy):
            term = jnp.where(lax.rem(gy + e, ngy) == b, got[e - 1], term)
        total = total + term
    for d in across:
        d.wait_send()
    for s in range(steps):
        pred[s] = total
        partner = gx + (1 << s) * (1 - 2 * lax.rem(gx // (1 << s), 2))
        swap = copy(pred.at[s], gxbuf.at[s], xs.at[s], xr.at[s], dev(partner, gy))
        swap.start()
        swap.wait()
        total = total + gxbuf[s]
    red_out[...] = total

    sent(geo_rows, has_dn, has_up)
    sent(geo_cols, has_rt, has_lf)
    for c in range(nc):
        sent(member_rows[c], has_dn, has_up)
        sent(member_cols[c], has_rt, has_lf)


PIVOTS = 4


def analysis_kernel(anom, mean, red, out):
    members = anom.shape[2]
    cx = anom.shape[1]
    half = members // 2
    wide = 2 * members
    packed = red[0:half]
    gram = jnp.concatenate([packed, roll(packed, members)], axis=0)
    lane = lanes((members, wide))
    row = lax.broadcasted_iota(jnp.int32, (members, wide), 0)
    aug = jnp.where(lane < members, gram, 0.0)
    aug = jnp.where((lane == row) | (lane == row + members), aug + 1.0, aug)
    tiles = [aug[8 * t : 8 * t + 8] for t in range(members // 8)]
    sub = lax.broadcasted_iota(jnp.int32, (8, wide), 0)
    for k0 in range(0, members, PIVOTS):
        t0, o = k0 // 8, k0 % 8
        cols = {
            t: [jnp.broadcast_to(tiles[t][:, k0 + j : k0 + j + 1], (8, wide)) for j in range(PIVOTS)]
            for t in range(t0, len(tiles))
        }
        rows = [tiles[t0][o + i : o + i + 1] for i in range(PIVOTS)]
        piv = [[cols[t0][j][o + i : o + i + 1] for j in range(PIVOTS)] for i in range(PIVOTS)]
        inv = []
        for j in range(PIVOTS):
            inv.append(1.0 / piv[j][j])
            for i in range(j + 1, PIVOTS):
                m = piv[i][j] * inv[j]
                rows[i] = rows[i] - m * rows[j]
                for q in range(j + 1, PIVOTS):
                    piv[i][q] = piv[i][q] - m * piv[j][q]
        for t in range(t0, len(tiles)):
            cur = cols[t]
            new = tiles[t]
            for j in range(PIVOTS):
                m = cur[j] * inv[j]
                if t == t0:
                    m = jnp.where(sub >= o + PIVOTS, m, 0.0)
                new = new - m * rows[j]
                for q in range(j + 1, PIVOTS):
                    cur[q] = cur[q] - m * piv[j][q]
            if t == t0:
                for i in range(PIVOTS):
                    new = jnp.where(sub == o + i, rows[i] * lax.rsqrt(piv[i][i]), new)
            tiles[t] = new
    linv = roll(jnp.concatenate(tiles, axis=0), members)[:, :members]
    proj = red[half : half + 1, :members]
    first = jnp.sum(linv * proj, axis=1, keepdims=True)
    weights = jnp.sum(linv * first, axis=0, keepdims=True)
    mix = linv + weights * (1.0 / math.sqrt(members - 1))
    for f in range(3):
        for x in range(cx):
            res = jnp.dot(mix, anom[f, x], precision=HIGH, preferred_element_type=F32)
            out[f, pl.ds(x, members, stride=cx), :] = res + mean[f, x : x + 1]


def local(ngx, ngy, members_state, depth_level, land_mask, obs_cells, obs_values, obs_error):
    _, members, cx, cy = members_state.shape
    obs = obs_cells.shape[-1]
    ext = cx + 2 * W
    nc = members // CHUNK
    steps = ngx.bit_length() - 1
    rows = members // 2 + 8
    vmem = pl.BlockSpec(memory_space=pltpu.VMEM)
    dma = pltpu.SemaphoreType.DMA
    anom, mean, red = pl.pallas_call(
        functools.partial(forecast_kernel, ngx, ngy),
        out_shape=(
            jax.ShapeDtypeStruct((3, cx, members, cy), F32),
            jax.ShapeDtypeStruct((3, cx, cy), F32),
            jax.ShapeDtypeStruct((rows, cy), F32),
        ),
        in_specs=[vmem] * 6,
        out_specs=(vmem,) * 3,
        scratch_shapes=[
            pltpu.VMEM((nc, ext, 3, CHUNK, cy), F32),
            pltpu.VMEM((ext, 3, CHUNK, cy), F32),
            pltpu.VMEM((ext, 3, CHUNK, cy), F32),
            pltpu.VMEM((ext, 2, 8, cy), F32),
            pltpu.VMEM((ext, 8, cy), F32),
            pltpu.VMEM((ext, 8, cy), F32),
            pltpu.VMEM((nc, 3, CHUNK, cy), F32),
            pltpu.VMEM((nc, 3, CHUNK, cy), F32),
            pltpu.VMEM((nc, 3, CHUNK, cy), F32),
            pltpu.VMEM((2, 8, cy), F32),
            pltpu.VMEM((2, 8, cy), F32),
            pltpu.VMEM((2, 8, cy), F32),
            pltpu.VMEM((2, 5, 8, cy), F32),
            pltpu.VMEM((rows, cy), F32),
            pltpu.VMEM((steps, rows, cy), F32),
            pltpu.VMEM((ngy - 1, rows, cy), F32),
            pltpu.VMEM((steps, rows, cy), F32),
            dma((nc, 2)), dma((nc, 2)), dma((nc, 2)), dma((nc, 2)),
            dma((2,)), dma((2,)), dma((2,)), dma((2,)),
            dma((ngy - 1,)), dma((ngy - 1,)), dma((steps,)), dma((steps,)),
        ],
        compiler_params=pltpu.CompilerParams(
            collective_id=0, has_side_effects=True, vmem_limit_bytes=40 * 2**20
        ),
    )(
        members_state.reshape(3, members * cx, cy), depth_level, land_mask,
        obs_cells.reshape(1, obs), obs_values.reshape(1, obs), obs_error.reshape(1, obs),
    )
    out = pl.pallas_call(
        analysis_kernel,
        out_shape=jax.ShapeDtypeStruct((3, members * cx, cy), F32),
        in_specs=[vmem] * 3,
        out_specs=vmem,
        compiler_params=pltpu.CompilerParams(vmem_limit_bytes=40 * 2**20),
    )(anom, mean, red)
    return out.reshape(members_state.shape)


def solution(mesh):
    placed = (
        P(None, None, "gx", "gy"),
        P("gx", "gy"),
        P("gx", "gy"),
        P("gx", "gy", None),
        P("gx", "gy", None),
        P("gx", "gy", None),
    )
    return jax.shard_map(
        functools.partial(local, mesh.shape["gx"], mesh.shape["gy"]),
        mesh=mesh, in_specs=placed, out_specs=P(None, None, "gx", "gy"), check_vma=False,
    )
```

```python
import functools
import math

import jax
import jax.numpy as jnp
from jax import lax
from jax.experimental import pallas as pl
from jax.experimental.pallas import tpu as pltpu
from jax.sharding import PartitionSpec as P

W = 3
CHUNK = 16
F32 = jnp.float32
HIGH = lax.Precision.HIGHEST
NT = (((1,), (1,)), ((), ()))


def lanes(shape):
    return lax.broadcasted_iota(jnp.int32, shape, 1)


def roll(a, by):
    by = by % a.shape[-1]
    return a if by == 0 else pltpu.roll(a, by, a.ndim - 1)


def pack(rows):
    out = jnp.zeros_like(rows[0])
    slot = lanes(out.shape) // 8
    for x, row in enumerate(rows):
        out = jnp.where(slot == x, roll(row, 8 * x + 4), out)
    return out


def west(c, strip, x):
    return jnp.where(lanes(c.shape) == 0, roll(strip, -(8 * x + 3)), roll(c, 1))


def east(c, strip, x):
    last = c.shape[1] - 1
    return jnp.where(lanes(c.shape) == last, roll(strip, last - (8 * x + 4)), roll(c, -1))


def tendency(c, up, dn, lf, rt, h_up, h_dn, h_lf, h_rt, mask):
    def lap(f):
        return up[f] + dn[f] + lf[f] + rt[f] - 4.0 * c[f]

    dh = -0.5 * (h_dn * dn[1] - h_up * up[1]) - 0.5 * (h_rt * rt[2] - h_lf * lf[2]) + 0.05 * lap(0)
    du = -0.5 * (dn[0] - up[0]) + 0.2 * c[2] + 0.05 * lap(1)
    dv = -0.5 * (rt[0] - lf[0]) - 0.2 * c[1] + 0.05 * lap(2)
    return dh * mask, du * mask, dv * mask


def forecast_kernel(
    ngx, ngy, state, depth, land, cells, values, error,
    anom_out, mean_out, red_out,
    y, z1, z2, geo, hl, hr, k, lk, rk, gk, glk, grk, sgeo, part, pred, got, gxbuf,
    row_s, row_r, col_s, col_r, grow_s, grow_r, gcol_s, gcol_r, ps, pr, xs, xr,
):
    members = state.shape[1] // depth.shape[0]
    cx = depth.shape[0]
    cy = depth.shape[1]
    ext = cx + 2 * W
    nc = members // CHUNK
    gx = lax.axis_index("gx")
    gy = lax.axis_index("gy")
    steps = ngx.bit_length() - 1

    def dev(a, b):
        return (a, b)

    bar = pltpu.get_barrier_semaphore()
    count = 0
    for target in (
        [dev(lax.rem(gx + 1, ngx), gy), dev(lax.rem(gx + ngx - 1, ngx), gy)]
        + [dev(gx, lax.rem(gy + d, ngy)) for d in range(1, ngy)]
        + [dev(gx + (1 << s) * (1 - 2 * (lax.rem(gx // (1 << s), 2))), gy) for s in range(steps)]
    ):
        pl.semaphore_signal(bar, inc=1, device_id=target, device_id_type=pl.DeviceIdType.MESH)
        count += 1

    maskf = land[...].astype(F32)
    heights = 0.25 * depth[...].astype(F32) * maskf
    for x in range(cx):
        geo[x + W, 0] = jnp.broadcast_to(heights[x : x + 1], (8, cy))
        geo[x + W, 1] = jnp.broadcast_to(maskf[x : x + 1], (8, cy))
    for c in range(nc):
        for f in range(3):
            for x in range(cx):
                y[c, x + W, f] = (
                    state[f, pl.ds(c * CHUNK * cx + x, CHUNK, stride=cx), :] * maskf[x : x + 1]
                )

    @pl.when(gx == 0)
    def _():
        y[:, 0:W] = jnp.zeros((nc, W, 3, CHUNK, cy), F32)
        geo[0:W] = jnp.zeros((W, 2, 8, cy), F32)

    @pl.when(gx == ngx - 1)
    def _():
        y[:, cx + W :] = jnp.zeros((nc, W, 3, CHUNK, cy), F32)
        geo[cx + W :] = jnp.zeros((W, 2, 8, cy), F32)

    @pl.when(gy == 0)
    def _():
        lk[...] = jnp.zeros(lk.shape, F32)
        glk[...] = jnp.zeros(glk.shape, F32)

    @pl.when(gy == ngy - 1)
    def _():
        rk[...] = jnp.zeros(rk.shape, F32)
        grk[...] = jnp.zeros(grk.shape, F32)

    pl.semaphore_wait(bar, count)

    def copy(src, dst, s, r, target):
        return pltpu.make_async_remote_copy(
            src_ref=src, dst_ref=dst, send_sem=s, recv_sem=r,
            device_id=target, device_id_type=pl.DeviceIdType.MESH,
        )

    below = dev(lax.rem(gx + 1, ngx), gy)
    above = dev(lax.rem(gx + ngx - 1, ngx), gy)
    right = dev(gx, lax.rem(gy + 1, ngy))
    left = dev(gx, lax.rem(gy + ngy - 1, ngy))
    has_up, has_dn = gx > 0, gx < ngx - 1
    has_lf, has_rt = gy > 0, gy < ngy - 1

    def rows_of(ref, s, r):
        return (
            copy(ref.at[pl.ds(cx, W)], ref.at[pl.ds(0, W)], s.at[0], r.at[0], below),
            copy(ref.at[pl.ds(W, W)], ref.at[pl.ds(cx + W, W)], s.at[1], r.at[1], above),
        )

    def cols_of(src, to_left, to_right, s, r):
        return (
            copy(src, to_left, s.at[0], r.at[0], right),
            copy(src, to_right, s.at[1], r.at[1], left),
        )

    def start(pair, first, second):
        pl.when(first)(lambda: pair[0].start())
        pl.when(second)(lambda: pair[1].start())

    def sent(pair, first, second):
        pl.when(first)(lambda: pair[0].wait_send())
        pl.when(second)(lambda: pair[1].wait_send())

    def received(pair, first, second):
        pl.when(second)(lambda: pair[0].wait_recv())
        pl.when(first)(lambda: pair[1].wait_recv())

    geo_rows = rows_of(geo, grow_s, grow_r)
    geo_cols = cols_of(gk, glk, grk, gcol_s, gcol_r)
    member_rows = [rows_of(y.at[c], row_s.at[c], row_r.at[c]) for c in range(nc)]
    member_cols = [cols_of(k.at[c], lk.at[c], rk.at[c], col_s.at[c], col_r.at[c]) for c in range(nc)]
    start(geo_rows, has_dn, has_up)
    for c in range(min(2, nc)):
        start(member_rows[c], has_dn, has_up)

    root = math.sqrt(members - 1)
    err = error[...]
    cell = cells[...]
    obs = cell.shape[1]
    weight = 1.0 / (err * err * root)
    row_at = cell // cy
    col_at = cell - row_at * cy
    sub = lax.broadcasted_iota(jnp.int32, (cx, obs), 0)
    here = sub == row_at
    by_row = jnp.concatenate(
        [jnp.where(here, weight, 0.0), jnp.where(here, weight * values[...], 0.0)], axis=0
    )
    hot = (lax.broadcasted_iota(jnp.int32, (cy, obs), 0) == col_at).astype(F32)
    sums = lax.dot_general(by_row, hot, NT, precision=HIGH, preferred_element_type=F32)
    s_cell, v_cell = sums[:cx], sums[cx:]

    received(geo_rows, has_dn, has_up)
    for f in range(2):
        gk[f] = pack([geo[x, f] for x in range(ext)])
    start(geo_cols, has_rt, has_lf)

    def strips(c):
        received(member_rows[c], has_dn, has_up)
        if c + 2 < nc:
            start(member_rows[c + 2], has_dn, has_up)
        for f in range(3):
            k[c, f] = pack([y[c, x, f] for x in range(ext)])
        start(member_cols[c], has_rt, has_lf)

    def sections(c):
        received(member_cols[c], has_rt, has_lf)
        first = lanes((CHUNK, cy)) % 8 < 4
        sl0 = [jnp.where(first, lk[c, f], k[c, f]) for f in range(3)]
        sr0 = [jnp.where(first, k[c, f], rk[c, f]) for f in range(3)]

        def strip_section(s, side):
            return tendency(
                s, [roll(a, 8) for a in s], [roll(a, -8) for a in s],
                [roll(a, 1) for a in s], [roll(a, -1) for a in s],
                sgeo[side, 0, 0:1], sgeo[side, 1, 0:1], sgeo[side, 2, 0:1], sgeo[side, 3, 0:1],
                sgeo[side, 4, 0:1],
            )

        def advance(s, side):
            d = strip_section(s, side)
            one = [s[f] + 0.3 * d[f] for f in range(3)]
            d = strip_section(one, side)
            two = [0.75 * s[f] + 0.25 * (one[f] + 0.3 * d[f]) for f in range(3)]
            return one, two

        sl1, sl2 = advance(sl0, 0)
        sr1, sr2 = advance(sr0, 1)

        def row_section(read, sl, sr, x):
            cc, up, dn = read(x), read(x - 1), read(x + 1)
            lf = [west(cc[f], sl[f], x) for f in range(3)]
            rt = [east(cc[f], sr[f], x) for f in range(3)]
            d = tendency(
                cc, up, dn, lf, rt, geo[x - 1, 0, 0:1], geo[x + 1, 0, 0:1],
                hl[x, 0:1], hr[x, 0:1], geo[x, 1, 0:1],
            )
            return cc, d

        for x in range(1, ext - 1):
            cc, d = row_section(lambda i: [y[c, i, f] for f in range(3)], sl0, sr0, x)
            for f in range(3):
                z1[x, f] = cc[f] + 0.3 * d[f]
        for x in range(2, ext - 2):
            cc, d = row_section(lambda i: [z1[i, f] for f in range(3)], sl1, sr1, x)
            for f in range(3):
                z2[x, f] = 0.75 * y[c, x, f] + 0.25 * (cc[f] + 0.3 * d[f])
        for x in range(3, ext - 3):
            cc, d = row_section(lambda i: [z2[i, f] for f in range(3)], sl2, sr2, x)
            for f in range(3):
                anom_out[f, x - W, c * CHUNK : (c + 1) * CHUNK] = (1.0 / 3.0) * y[c, x, f] + (
                    2.0 / 3.0
                ) * (cc[f] + 0.3 * d[f])

    strips(0)
    received(geo_cols, has_rt, has_lf)
    first = lanes((8, cy)) % 8 < 4
    gl = [jnp.where(first, glk[f], gk[f]) for f in range(2)]
    gr = [jnp.where(first, gk[f], grk[f]) for f in range(2)]
    for side, g in ((0, gl), (1, gr)):
        sgeo[side, 0] = roll(g[0], 8)
        sgeo[side, 1] = roll(g[0], -8)
        sgeo[side, 2] = roll(g[0], 1)
        sgeo[side, 3] = roll(g[0], -1)
        sgeo[side, 4] = g[1]
    for x in range(ext):
        hl[x] = west(geo[x, 0], gl[0], x)
        hr[x] = east(geo[x, 0], gr[0], x)
    for c in range(nc):
        if c + 1 < nc:
            strips(c + 1)
        sections(c)

    gram = jnp.zeros((members + 8, members), F32)
    for f in range(3):
        for x in range(cx):
            full = anom_out[f, x]
            mean = jnp.sum(full, axis=0, keepdims=True) * (1.0 / members)
            mean_out[f, x : x + 1] = mean
            full = full - mean
            anom_out[f, x] = full
            if f == 0:
                wide = full * (s_cell[x : x + 1] * (1.0 / root))
                proj = jnp.broadcast_to(v_cell[x : x + 1] - s_cell[x : x + 1] * mean, (8, cy))
                lhs = jnp.concatenate([wide, proj], axis=0)
                gram += lax.dot_general(lhs, full, NT, precision=HIGH, preferred_element_type=F32)
    half = members // 2
    part[0:half] = jnp.concatenate([gram[:half], gram[half:members]], axis=1)
    part[half:] = jnp.concatenate([gram[members:], gram[members:]], axis=1)

    across = [
        copy(part, got.at[ngy - d - 1], ps.at[d - 1], pr.at[ngy - d - 1], dev(gx, lax.rem(gy + d, ngy)))
        for d in range(1, ngy)
    ]
    for d in across:
        d.start()
    for d in across:
        d.wait_recv()
    total = jnp.zeros(part.shape, F32)
    for b in range(ngy):
        term = part[...]
        for e in range(1, ngy):
            term = jnp.where(lax.rem(gy + e, ngy) == b, got[e - 1], term)
        total = total + term
    for d in across:
        d.wait_send()
    for s in range(steps):
        pred[s] = total
        partner = gx + (1 << s) * (1 - 2 * lax.rem(gx // (1 << s), 2))
        swap = copy(pred.at[s], gxbuf.at[s], xs.at[s], xr.at[s], dev(partner, gy))
        swap.start()
        swap.wait()
        total = total + gxbuf[s]
    red_out[...] = total

    sent(geo_rows, has_dn, has_up)
    sent(geo_cols, has_rt, has_lf)
    for c in range(nc):
        sent(member_rows[c], has_dn, has_up)
        sent(member_cols[c], has_rt, has_lf)


PIVOTS = 4


def analysis_kernel(anom, mean, red, out):
    members = anom.shape[2]
    cx = anom.shape[1]
    half = members // 2
    wide = 2 * members
    packed = red[0:half]
    gram = jnp.concatenate([packed, roll(packed, members)], axis=0)
    lane = lanes((members, wide))
    row = lax.broadcasted_iota(jnp.int32, (members, wide), 0)
    aug = jnp.where(lane < members, gram, 0.0)
    aug = jnp.where((lane == row) | (lane == row + members), aug + 1.0, aug)
    tiles = [aug[8 * t : 8 * t + 8] for t in range(members // 8)]
    sub = lax.broadcasted_iota(jnp.int32, (8, wide), 0)
    for k0 in range(0, members, PIVOTS):
        t0, o = k0 // 8, k0 % 8
        cols = {
            t: [jnp.broadcast_to(tiles[t][:, k0 + j : k0 + j + 1], (8, wide)) for j in range(PIVOTS)]
            for t in range(t0, len(tiles))
        }
        rows = [tiles[t0][o + i : o + i + 1] for i in range(PIVOTS)]
        piv = [[cols[t0][j][o + i : o + i + 1] for j in range(PIVOTS)] for i in range(PIVOTS)]
        inv = []
        for j in range(PIVOTS):
            inv.append(1.0 / piv[j][j])
            for i in range(j + 1, PIVOTS):
                m = piv[i][j] * inv[j]
                rows[i] = rows[i] - m * rows[j]
                for q in range(j + 1, PIVOTS):
                    piv[i][q] = piv[i][q] - m * piv[j][q]
        for t in range(t0, len(tiles)):
            cur = cols[t]
            new = tiles[t]
            for j in range(PIVOTS):
                m = cur[j] * inv[j]
                if t == t0:
                    m = jnp.where(sub >= o + PIVOTS, m, 0.0)
                new = new - m * rows[j]
                for q in range(j + 1, PIVOTS):
                    cur[q] = cur[q] - m * piv[j][q]
            if t == t0:
                for i in range(PIVOTS):
                    new = jnp.where(sub == o + i, rows[i] * lax.rsqrt(piv[i][i]), new)
            tiles[t] = new
    linv = roll(jnp.concatenate(tiles, axis=0), members)[:, :members]
    proj = red[half : half + 1, :members]
    first = jnp.sum(linv * proj, axis=1, keepdims=True)
    weights = jnp.sum(linv * first, axis=0, keepdims=True)
    mix = linv + weights * (1.0 / math.sqrt(members - 1))
    for f in range(3):
        for x in range(cx):
            res = jnp.dot(mix, anom[f, x], precision=HIGH, preferred_element_type=F32)
            out[f, pl.ds(x, members, stride=cx), :] = res + mean[f, x : x + 1]


def local(ngx, ngy, members_state, depth_level, land_mask, obs_cells, obs_values, obs_error):
    _, members, cx, cy = members_state.shape
    obs = obs_cells.shape[-1]
    ext = cx + 2 * W
    nc = members // CHUNK
    steps = ngx.bit_length() - 1
    rows = members // 2 + 8
    vmem = pl.BlockSpec(memory_space=pltpu.VMEM)
    dma = pltpu.SemaphoreType.DMA
    anom, mean, red = pl.pallas_call(
        functools.partial(forecast_kernel, ngx, ngy),
        out_shape=(
            jax.ShapeDtypeStruct((3, cx, members, cy), F32),
            jax.ShapeDtypeStruct((3, cx, cy), F32),
            jax.ShapeDtypeStruct((rows, cy), F32),
        ),
        in_specs=[vmem] * 6,
        out_specs=(vmem,) * 3,
        scratch_shapes=[
            pltpu.VMEM((nc, ext, 3, CHUNK, cy), F32),
            pltpu.VMEM((ext, 3, CHUNK, cy), F32),
            pltpu.VMEM((ext, 3, CHUNK, cy), F32),
            pltpu.VMEM((ext, 2, 8, cy), F32),
            pltpu.VMEM((ext, 8, cy), F32),
            pltpu.VMEM((ext, 8, cy), F32),
            pltpu.VMEM((nc, 3, CHUNK, cy), F32),
            pltpu.VMEM((nc, 3, CHUNK, cy), F32),
            pltpu.VMEM((nc, 3, CHUNK, cy), F32),
            pltpu.VMEM((2, 8, cy), F32),
            pltpu.VMEM((2, 8, cy), F32),
            pltpu.VMEM((2, 8, cy), F32),
            pltpu.VMEM((2, 5, 8, cy), F32),
            pltpu.VMEM((rows, cy), F32),
            pltpu.VMEM((steps, rows, cy), F32),
            pltpu.VMEM((ngy - 1, rows, cy), F32),
            pltpu.VMEM((steps, rows, cy), F32),
            dma((nc, 2)), dma((nc, 2)), dma((nc, 2)), dma((nc, 2)),
            dma((2,)), dma((2,)), dma((2,)), dma((2,)),
            dma((ngy - 1,)), dma((ngy - 1,)), dma((steps,)), dma((steps,)),
        ],
        compiler_params=pltpu.CompilerParams(
            collective_id=0, has_side_effects=True, vmem_limit_bytes=40 * 2**20
        ),
    )(
        members_state.reshape(3, members * cx, cy), depth_level, land_mask,
        obs_cells.reshape(1, obs), obs_values.reshape(1, obs), obs_error.reshape(1, obs),
    )
    out = pl.pallas_call(
        analysis_kernel,
        out_shape=jax.ShapeDtypeStruct((3, members * cx, cy), F32),
        in_specs=[vmem] * 3,
        out_specs=vmem,
        compiler_params=pltpu.CompilerParams(vmem_limit_bytes=40 * 2**20),
    )(anom, mean, red)
    return out.reshape(members_state.shape)


def solution(mesh):
    placed = (
        P(None, None, "gx", "gy"),
        P("gx", "gy"),
        P("gx", "gy"),
        P("gx", "gy", None),
        P("gx", "gy", None),
        P("gx", "gy", None),
    )
    return jax.shard_map(
        functools.partial(local, mesh.shape["gx"], mesh.shape["gy"]),
        mesh=mesh, in_specs=placed, out_specs=P(None, None, "gx", "gy"), check_vma=False,
    )
```
